512 devices in a mesh: dp: 64 (over z, y), mp: 8 (over x, core).
Axes of the slice: x: 4, y: 4, z: 16, core: 2. Of those that a mesh axis runs over, the one named last changes fastest.
Arguments:
- query_raw: bfloat16 [8192, 1024], P('dp', 'mp'), may hold values from -4 to 4
- key_raw: bfloat16 [8192, 1024], P('dp', 'mp'), may hold values from -4 to 4
- values: bfloat16 [8192, 2048], P('dp', 'mp'), may hold values from -8 to 8
- decay_input: float32 [8192, 16], P('dp', 'mp'), may hold values from -4 to 4
- beta_input: float32 [8192, 16], P('dp', 'mp'), may hold values from -6 to 6
- log_rate: float32 [16], P('mp'), may hold values from -3 to 1
- step_bias: float32 [16], P('mp'), may hold values from -2 to 1
- gain: float32 [128], replicated, may hold values from 0.5 to 1.5
- out_weight: bfloat16 [2048, 2048], P('mp'), may hold values from -0.125 to 0.125
- upstream: bfloat16 [8192, 2048], P('dp'), may hold values from -0.1875 to 0.1875
Outputs:
- weight_grad: bfloat16 [2048, 2048], P('mp')
- gain_grad: float32 [128], replicated
- decay_grad: float32 [16], replicated
The draws below stay inside these ranges and needn't reach their ends.
All inputs are finite; a program needn't handle non-finite values.
Results may differ from the reference program's by a relative error of at most 0.0033.
Values may be sent and summed in bfloat16 or wider, within the bound.
No kernel may reach another device: no remote copies, remote signals or barrier semaphores. Data moves between devices by JAX's collectives and lax.ppermute only.
A program may use at most 64 MiB of HBM per device.

```python
import math
import jax
import jax.numpy as jnp
from jax import lax

D = 2048
HD = 128
QKH = 8
VH = 16
SPAN = 64
TOK_DEV = 128
TOKENS = 8192
VDIM = 2048
N_DP = 64


def noise(key, shape):
    normal = jax.random.normal(jax.random.fold_in(key, 7), shape, jnp.float32)
    return normal


def replica_mix(key, width, shared):
    common = noise(jax.random.fold_in(key, 1), (TOK_DEV, width))
    own = noise(jax.random.fold_in(key, 2), (N_DP, TOK_DEV, width))
    return (common[None] + own) / math.sqrt(1.0 + shared)


def draw_query_raw(key, part):
    key = jax.random.fold_in(key, 11)
    mixed = replica_mix(key, QKH * HD, 1.0)
    return jnp.clip(mixed, -4.0, 4.0).reshape(TOKENS, QKH * HD).astype(jnp.bfloat16)


def draw_key_raw(key, part):
    key = jax.random.fold_in(key, 12)
    mixed = replica_mix(key, QKH * HD, 1.0)
    return jnp.clip(mixed, -4.0, 4.0).reshape(TOKENS, QKH * HD).astype(jnp.bfloat16)


def draw_values(key, part):
    key = jax.random.fold_in(key, 13)
    mixed = replica_mix(key, VDIM, 1.0)
    head_scale = jnp.repeat(3.0 ** (jnp.arange(VH, dtype=jnp.float32) / (VH - 1)), HD)
    return jnp.clip(mixed * head_scale, -8.0, 8.0).reshape(TOKENS, VDIM).astype(jnp.bfloat16)


def draw_upstream(key, part):
    key = jax.random.fold_in(key, 14)
    mixed = replica_mix(key, D, 1.0)
    column_scale = jnp.exp(jax.random.uniform(jax.random.fold_in(key, 3), (D,), jnp.float32, 0.0, math.log(10.0)))
    replica_scale = 3.0 ** (jnp.arange(N_DP, dtype=jnp.float32) / (N_DP - 1))
    scaled = mixed * column_scale[None, None, :] * replica_scale[:, None, None]
    return (jnp.clip(scaled, -12.0, 12.0) / 64.0).reshape(TOKENS, D).astype(jnp.bfloat16)


def shard_levels(rng, extent, cuts, low, high):
    loudness, own = 1.0, jax.random.fold_in(rng, 6)
    for dim, blocks in cuts:
        steps = jnp.exp(jax.random.uniform(jax.random.fold_in(own, dim), (blocks,), jnp.float32, low / len(cuts), high / len(cuts)))
        loudness = loudness * jnp.repeat(steps, extent[dim] // blocks).reshape([-1 if axis == dim else 1 for axis in range(len(extent))])
    return loudness


def centred(rng, dims, scale, bound, cuts=(), kind=jnp.bfloat16):
    factor_of = shard_levels(rng, dims, cuts, -0.22, 0.18) if cuts else 1.0
    values = jax.random.normal(rng, dims, jnp.float32) * scale * factor_of
    return jnp.minimum(jnp.maximum(values, -bound), bound).astype(kind)


def setup_inputs(seed: int = 0) -> dict:
    seeds = jax.random.split(jax.random.key(seed), 11)
    query_raw = draw_query_raw(jax.random.fold_in(seeds[10], 71), 0)
    key_raw = draw_key_raw(jax.random.fold_in(seeds[10], 71), 0)
    values = draw_values(jax.random.fold_in(seeds[10], 71), 0)
    decay_input = centred(seeds[3], (TOKENS, VH), 1.0, 4.0, ((0, 64), (1, 8)), jnp.float32)
    beta_input = centred(seeds[4], (TOKENS, VH), 1.5, 6.0, ((0, 64), (1, 8)), jnp.float32)
    log_rate = jnp.clip(-3.0 + 4.0 * jax.random.uniform(seeds[5], (VH,), jnp.float32) ** shard_levels(seeds[5], (VH,), ((0, 8),), -0.2, 0.2), -3.0, 1.0)
    step_bias = jnp.clip(-2.0 + 3.0 * jax.random.uniform(seeds[6], (VH,), jnp.float32) ** shard_levels(seeds[6], (VH,), ((0, 8),), -0.2, 0.2), -2.0, 1.0)
    gain = jnp.clip(1.0 + 0.1 * jax.random.normal(seeds[7], (HD,), jnp.float32), 0.5, 1.5)
    out_weight = centred(seeds[8], (VDIM, D), VDIM ** -0.5, 0.125, ((0, 8),))
    upstream = draw_upstream(jax.random.fold_in(seeds[10], 71), 0)
    return {"query_raw": query_raw, "key_raw": key_raw, "values": values, "decay_input": decay_input, "beta_input": beta_input, "log_rate": log_rate, "step_bias": step_bias, "gain": gain, "out_weight": out_weight, "upstream": upstream}


EPS = 1e-06
HIGH = lax.Precision.HIGHEST

def unit_rows(raw, heads):
    count = raw.shape[0]
    shaped = raw.astype(jnp.float32).reshape(count, heads, -1)
    return shaped / jnp.sqrt(lax.optimization_barrier(jnp.sum(shaped * shaped, axis=-1, keepdims=True)) + EPS)

def span_step(state, block):
    query, keys, vals, log_decay, beta = block
    width = query.shape[-1]
    count = log_decay.shape[-1]
    places = jnp.arange(count)
    lower = places[:, None] >= places[None, :]
    strict = places[:, None] > places[None, :]
    cumul = jnp.cumsum(log_decay, axis=1)
    spread = cumul[:, :, None] - cumul[:, None, :]
    decay = jnp.where(lower, jnp.exp(jnp.where(lower, spread, 0.0)), 0.0)
    inner = jnp.einsum('hid,hjd->hij', keys, keys, precision=HIGH)
    coupling = jnp.where(strict, beta[:, :, None] * inner * decay, 0.0)
    system = coupling + jnp.eye(count, dtype=log_decay.dtype)
    growth = jnp.exp(cumul)
    right = jnp.concatenate([beta[:, :, None] * vals, (beta * growth)[:, :, None] * keys], axis=2)
    solved = jax.scipy.linalg.solve_triangular(system, right, lower=True, unit_diagonal=True)
    writes = solved[:, :, :width] - jnp.einsum('hcd,hde->hce', solved[:, :, width:], state, precision=HIGH)
    scores = jnp.einsum('hid,hjd->hij', query, keys, precision=HIGH) * decay
    output = growth[:, :, None] * jnp.einsum('hcd,hde->hce', query, state, precision=HIGH)
    output = output + jnp.einsum('hij,hje->hie', scores, writes, precision=HIGH)
    final = cumul[:, -1]
    weighted = keys * jnp.exp(final[:, None] - cumul)[:, :, None]
    carried = jnp.exp(final)[:, None, None] * state + jnp.einsum('hcd,hce->hde', weighted, writes, precision=HIGH)
    return (carried, output)

def delta_rule(query, keys, vals, log_decay, beta):
    count, heads, width = vals.shape
    blocks = count // SPAN

    def split(array):
        shaped = array.reshape((blocks, SPAN) + array.shape[1:])
        return jnp.swapaxes(shaped, 1, 2)
    start = jnp.zeros((heads, width, width), vals.dtype)
    ending, outputs = lax.scan(span_step, start, (split(query), split(keys), split(vals), split(log_decay), split(beta)))
    return jnp.swapaxes(outputs, 1, 2).reshape(count, heads, width)

def layer_forward(query_raw, key_raw, values, decay_input, beta_input, log_rate, step_bias, gain):
    width = gain.shape[0]
    qk_heads = query_raw.shape[1] // width
    heads = log_rate.shape[0]
    count = values.shape[0]
    repeat = heads // qk_heads
    query = jnp.repeat(unit_rows(query_raw, qk_heads) * width ** (-0.5), repeat, axis=1)
    keys = jnp.repeat(unit_rows(key_raw, qk_heads), repeat, axis=1)
    vals = values.astype(jnp.float32).reshape(count, heads, width)
    log_decay = -jnp.exp(log_rate)[None, :] * jax.nn.softplus(decay_input + step_bias[None, :])
    beta = jax.nn.sigmoid(beta_input)
    mixed = delta_rule(query, keys, vals, log_decay, beta)
    scale = lax.rsqrt(lax.optimization_barrier(jnp.mean(mixed * mixed, axis=-1, keepdims=True)) + EPS)
    return (mixed * scale * gain).reshape(count, heads * width)

def pair_combine(first, second):
    inner = jnp.sum(first * second)
    first_norm = jnp.sum(first * first) + EPS
    second_norm = jnp.sum(second * second) + EPS
    return (1.0 - inner / (2.0 * first_norm)) * first + (1.0 - inner / (2.0 * second_norm)) * second

def adasum_tree(stack):
    while stack.shape[0] > 1:
        half = stack.shape[0] // 2
        stack = jax.vmap(pair_combine)(stack[:half], stack[half:])
    return stack[0]

def reference(query_raw, key_raw, values, decay_input, beta_input, log_rate, step_bias, gain, out_weight, upstream):

    def replica(index):
        start = index * TOK_DEV

        def rows_of(array):
            return lax.dynamic_slice_in_dim(array, start, TOK_DEV, 0)
        grad_out = rows_of(upstream)

        def forward(rates, gains):
            return layer_forward(rows_of(query_raw), rows_of(key_raw), rows_of(values), rows_of(decay_input), rows_of(beta_input), rates, step_bias, gains)
        normed, pull = jax.vjp(forward, log_rate, gain)
        grad_w = lax.dot_general(normed.astype(jnp.bfloat16).astype(jnp.float32), grad_out.astype(jnp.float32), (((0,), (0,)), ((), ())), preferred_element_type=jnp.float32)
        d_normed = lax.dot_general(grad_out.astype(jnp.float32), out_weight.astype(jnp.float32), (((1,), (1,)), ((), ())), preferred_element_type=jnp.float32)
        grad_rate, grad_gain = pull(d_normed)
        return (grad_w, grad_gain, grad_rate)
    grads_w, grads_gain, grads_rate = lax.map(replica, jnp.arange(N_DP, dtype=jnp.int32))
    return (adasum_tree(grads_w).astype(jnp.bfloat16), adasum_tree(grads_gain), adasum_tree(grads_rate))
```

```python
import functools

import jax
import jax.numpy as jnp
from jax import lax
from jax.experimental import pallas as pl
from jax.experimental.pallas import tpu as pltpu
from jax.sharding import PartitionSpec as P

EPS = 1e-06
F32 = jnp.float32
BF16 = jnp.bfloat16
HIGH = lax.Precision.HIGHEST
TOK = 128
HD = 128
HEADS = 2
REPS = 64
N_Z = 16
N_Y = 4
N_MP = 8
TILE = 64
LIMIT = 48 * 1024 * 1024
NN = (((1,), (0,)), ((), ()))
NT = (((1,), (1,)), ((), ()))

Z_GROUPS = [[z * N_Y + y for z in range(N_Z)] for y in range(N_Y)]
Y_GROUPS = [[z * N_Y + y for y in range(N_Y)] for z in range(N_Z)]


def matmul(a, b, dims=NN):
    return lax.dot_general(a, b, dims, precision=HIGH, preferred_element_type=F32)


def places(shape):
    return (
        lax.broadcasted_iota(jnp.int32, shape, 0),
        lax.broadcasted_iota(jnp.int32, shape, 1),
    )


def unit_rows(raw):
    value = raw.astype(F32)
    return value / jnp.sqrt(jnp.sum(value * value, axis=-1, keepdims=True) + EPS)


def invert_all(systems):
    row, col = places((TOK, TOK))
    eye = (row == col).astype(F32)
    close = (row >> 3) == (col >> 3)
    first = [jnp.where(close, low, 0.0) for low in systems]
    second = [matmul(a, a) for a in first]
    fourth = [matmul(a, a) for a in second]
    out = [eye - a for a in first]
    out = [a + matmul(a, b) for a, b in zip(out, second)]
    out = [a + matmul(a, b) for a, b in zip(out, fourth)]
    for shift in (3, 4, 5, 6):
        off = ((row >> (shift + 1)) == (col >> (shift + 1))) & ((row >> shift) != (col >> shift))
        parts = [matmul(jnp.where(off, low, 0.0), a) for low, a in zip(systems, out)]
        out = [a - matmul(a, b) for a, b in zip(out, parts)]
    return out


def forward_kernel(
    q_ref, k_ref, v_ref, dec_ref, beta_ref, rate_ref, bias_ref, gain_ref, up_ref,
    g_ref, m_ref, l_ref, s_ref, a_ref, w_ref, o_ref,
):
    row, col = places((TOK, TOK))
    lower = row >= col
    strict = row > col
    query = unit_rows(q_ref[...]) * HD ** (-0.5)
    keys = unit_rows(k_ref[...])
    inner = matmul(keys, keys, NT)
    scores = matmul(query, keys, NT)
    pre = dec_ref[...] + bias_ref[...]
    soft = jnp.maximum(pre, 0.0) + jnp.log1p(jnp.exp(-jnp.abs(pre)))
    log_decay = -jnp.exp(rate_ref[...]) * soft
    beta = 1.0 / (1.0 + jnp.exp(-beta_ref[...]))
    cumul = matmul(lower.astype(F32), log_decay)
    mixers, systems = [], []
    for h in range(HEADS):
        wide = jnp.broadcast_to(cumul[:, h : h + 1], (TOK, TOK))
        spread = jnp.where(lower, wide - wide.T, 0.0)
        decay = jnp.where(lower, jnp.exp(spread), 0.0)
        mixers.append(scores * decay)
        systems.append(jnp.where(strict, beta[:, h : h + 1] * inner * decay, 0.0))
        m_ref[h] = mixers[h]
        l_ref[h] = systems[h]
        s_ref[h] = spread
    inverses = invert_all(systems)
    writes = [
        matmul(inverses[h], beta[:, h : h + 1] * v_ref[:, h * HD : (h + 1) * HD].astype(F32))
        for h in range(HEADS)
    ]
    mixed = [matmul(mixers[h], writes[h]) for h in range(HEADS)]
    normed = []
    for h in range(HEADS):
        a_ref[h] = inverses[h]
        w_ref[h] = writes[h]
        o_ref[h] = mixed[h]
        scale = lax.rsqrt(jnp.mean(mixed[h] * mixed[h], axis=-1, keepdims=True) + EPS)
        normed.append((mixed[h] * scale * gain_ref[...]).T.astype(BF16))
    left = jnp.concatenate(normed, axis=0)
    for z in range(N_Z):
        part = lax.dot_general(
            left, up_ref[:, z * HD : (z + 1) * HD], NN, preferred_element_type=F32
        ).astype(BF16)
        for y in range(N_Y):
            g_ref[z * N_Y + y] = part[y * TILE : (y + 1) * TILE, :]


def backward_kernel(
    place_ref, m_ref, l_ref, s_ref, a_ref, w_ref, o_ref, gain_ref, weight_ref, up_ref, out_ref
):
    gain = gain_ref[...]
    d_normed = lax.dot_general(up_ref[...], weight_ref[...], NT, preferred_element_type=F32)
    lane = lax.broadcasted_iota(jnp.int32, (1, HD), 1)
    heads = range(HEADS)
    turns = [matmul(l_ref[h] * s_ref[h], w_ref[h]) for h in heads]
    turns = [matmul(a_ref[h], turns[h]) for h in heads]
    slopes = [matmul(m_ref[h] * s_ref[h], w_ref[h]) - matmul(m_ref[h], turns[h]) for h in heads]
    grad_gain = jnp.zeros((1, HD), F32)
    rates = jnp.zeros((1, HD), F32)
    for h in heads:
        mixed = o_ref[h]
        scale = lax.rsqrt(jnp.mean(mixed * mixed, axis=-1, keepdims=True) + EPS)
        unit = mixed * scale
        given = d_normed[:, h * HD : (h + 1) * HD]
        grad_gain = grad_gain + jnp.sum(unit * given, axis=0, keepdims=True)
        tilted = given * gain
        d_mixed = scale * (tilted - unit * jnp.mean(unit * tilted, axis=-1, keepdims=True))
        rate = jnp.sum(jnp.sum(d_mixed * slopes[h], axis=0, keepdims=True), axis=1, keepdims=True)
        rates = rates + jnp.where(lane == place_ref[0] * HEADS + h, rate, 0.0)
    out_ref[...] = jnp.concatenate([grad_gain, rates], axis=0)


def gram_kernel(x_ref, small_ref, out_ref, wide):
    wide[...] = x_ref[...].astype(F32).reshape(REPS * TILE, HD)
    total = jnp.zeros((REPS, REPS), F32)
    for f in range(0, TILE, 2):
        rows = jnp.concatenate(
            [wide[pl.ds(f + e, REPS, stride=TILE), :].astype(BF16) for e in range(2)], axis=1
        )
        total = total + lax.dot_general(rows, rows, NT, preferred_element_type=F32)
    half = jnp.concatenate([total[: REPS // 2], total[REPS // 2 :]], axis=1)
    small = small_ref[...]
    fill = jnp.zeros((2, HD), F32)
    for m in range(N_MP):
        out_ref[m] = jnp.concatenate([half[4 * m : 4 * m + 4], small, fill], axis=0)


def spread_kernel(in_ref, out_ref):
    total = in_ref[0]
    for m in range(1, N_MP):
        total = total + in_ref[m]
    out_ref[...] = jnp.broadcast_to(total[None], out_ref.shape)


def small_tree(stack):
    half = REPS // 2
    while half:
        other = pltpu.roll(stack, half, 0)
        inner = jnp.sum(stack * other, axis=1, keepdims=True)
        norm = jnp.sum(stack * stack, axis=1, keepdims=True)
        part = (1.0 - inner / (2.0 * (norm + EPS))) * stack
        stack = part + pltpu.roll(part, half, 0)
        half //= 2
    return stack[0:1]


def gather_kernel(in_ref, gram_ref, gain_ref, rate_ref):
    total = in_ref[0, 0:4]
    for r in range(1, REPS):
        total = total + in_ref[r, 0:4]
    gram_ref[...] = jnp.broadcast_to(total[None], gram_ref.shape)
    flat = in_ref[...].reshape(REPS * 8, HD)
    gains = jnp.concatenate([flat[8 * r + 4 : 8 * r + 5] for r in range(REPS)], axis=0)
    rates = jnp.concatenate([flat[8 * r + 5 : 8 * r + 6] for r in range(REPS)], axis=0)
    gain_ref[...] = small_tree(gains)
    rate_ref[...] = small_tree(rates)


def path_coefs(gram):
    row, lane = places((REPS, HD))
    same = row == (lane & (REPS - 1))
    near = row == lane
    coefs = jnp.ones((REPS, 1), F32)
    half = REPS // 2
    while half:
        other = pltpu.roll(gram, half, 1)
        norm_col = jnp.sum(jnp.where(near, gram, 0.0), axis=1, keepdims=True)
        inner_col = jnp.sum(jnp.where(near, other, 0.0), axis=1, keepdims=True)
        norm_row = jnp.sum(jnp.where(same, gram, 0.0), axis=0, keepdims=True)
        inner_row = jnp.sum(jnp.where(same, other, 0.0), axis=0, keepdims=True)
        by_col = 1.0 - inner_col / (2.0 * (norm_col + EPS))
        by_row = 1.0 - inner_row / (2.0 * (norm_row + EPS))
        coefs = coefs * by_col
        part = by_col * by_row * gram
        part = part + pltpu.roll(part, half, 1)
        gram = part + pltpu.roll(part, half, 0)
        half //= 2
    return coefs


def combine_kernel(gram_ref, x_ref, out_ref, factor):
    lane = lax.broadcasted_iota(jnp.int32, (REPS // 2, HD), 1)
    packed = gram_ref[...].reshape(REPS // 2, HD)
    turned = pltpu.roll(packed, REPS, 1)
    gram = jnp.concatenate(
        [jnp.where(lane < REPS, packed, turned), jnp.where(lane < REPS, turned, packed)], axis=0
    )
    factor[...] = jnp.broadcast_to(path_coefs(gram), (REPS, HD))
    total = jnp.zeros((TILE, HD), F32)
    for r in range(REPS):
        total = total + factor[r : r + 1, :] * x_ref[r].astype(F32)
    out_ref[...] = jnp.broadcast_to(total.astype(BF16)[None], out_ref.shape)


def call(body, outs, ops, scratch=(), smem=(), flops=0):
    size = sum(o.size * o.dtype.itemsize for o in ops) + sum(o.size * o.dtype.itemsize for o in outs)
    specs = [
        pl.BlockSpec(memory_space=pltpu.SMEM if i in smem else pltpu.VMEM) for i in range(len(ops))
    ]
    return pl.pallas_call(
        body,
        out_shape=outs,
        in_specs=specs,
        out_specs=[pl.BlockSpec(memory_space=pltpu.VMEM) for _ in outs],
        scratch_shapes=list(scratch),
        compiler_params=pltpu.CompilerParams(vmem_limit_bytes=LIMIT),
        cost_estimate=pl.CostEstimate(flops=flops, bytes_accessed=size, transcendentals=0),
    )(*ops)


def shape(dims, dtype=F32):
    return jax.ShapeDtypeStruct(dims, dtype)


def per_device(
    query_raw, key_raw, values, decay_input, beta_input, log_rate, step_bias, gain, out_weight, upstream
):
    gain_row = gain[None, :]
    square = shape((HEADS, TOK, TOK))
    tiles, *saved = call(
        forward_kernel,
        [shape((REPS, TILE, HD), BF16)] + [square] * 6,
        [
            query_raw, key_raw, values, decay_input, beta_input,
            log_rate[None, :], step_bias[None, :], gain_row, upstream,
        ],
        flops=2 * 10**9,
    )
    stack = lax.all_to_all(tiles, "dp", 0, 0)
    place = lax.axis_index("mp").astype(jnp.int32)[None]
    (small,) = call(
        backward_kernel,
        [shape((2, HD))],
        [place, *saved, gain_row, out_weight, upstream],
        smem=(0,),
        flops=2 * 10**9,
    )
    (gram_part,) = call(
        gram_kernel,
        [shape((N_MP, 8, HD))],
        [stack, small],
        scratch=[pltpu.VMEM((REPS * TILE, HD), F32)],
        flops=10**9,
    )
    gram_part = lax.all_to_all(gram_part, "mp", 0, 0)
    (gram_part,) = call(spread_kernel, [shape((REPS, 8, HD))], [gram_part])
    gram_part = lax.all_to_all(gram_part, "dp", 0, 0)
    gram_part, gain_final, rate_final = call(
        gather_kernel, [shape((N_MP, 4, HD)), shape((1, HD)), shape((1, HD))], [gram_part]
    )
    gram = lax.all_to_all(gram_part, "mp", 0, 0)
    (whole,) = call(
        combine_kernel,
        [shape((N_Z, TILE, HD), BF16)],
        [gram, stack],
        scratch=[pltpu.VMEM((REPS, HD), F32)],
        flops=10**8,
    )
    whole = lax.all_to_all(whole, "dp", 0, 0, axis_index_groups=Z_GROUPS)
    whole = jnp.broadcast_to(whole[None], (N_Y,) + whole.shape)
    whole = lax.all_to_all(whole, "dp", 0, 0, axis_index_groups=Y_GROUPS)
    whole = jnp.transpose(whole, (0, 2, 1, 3)).reshape(N_Y * TILE, N_Z * HD)
    return (whole, gain_final[0], rate_final[0, : HEADS * N_MP])


def solution(mesh):
    in_specs = (
        P("dp", "mp"),
        P("dp", "mp"),
        P("dp", "mp"),
        P("dp", "mp"),
        P("dp", "mp"),
        P("mp"),
        P("mp"),
        P(),
        P("mp", None),
        P("dp", None),
    )
    out_specs = (P("mp", None), P(), P())
    return jax.shard_map(
        per_device, mesh=mesh, in_specs=in_specs, out_specs=out_specs, check_vma=False
    )
```

```python
import functools

import jax
import jax.numpy as jnp
from jax import lax
from jax.experimental import pallas as pl
from jax.experimental.pallas import tpu as pltpu
from jax.sharding import PartitionSpec as P

EPS = 1e-06
F32 = jnp.float32
BF16 = jnp.bfloat16
HIGH = lax.Precision.HIGHEST
TOK = 128
HD = 128
HEADS = 2
REPS = 64
N_Z = 16
N_Y = 4
N_MP = 8
TILE = 64
LIMIT = 48 * 1024 * 1024
NN = (((1,), (0,)), ((), ()))
NT = (((1,), (1,)), ((), ()))

Z_GROUPS = [[z * N_Y + y for z in range(N_Z)] for y in range(N_Y)]
Y_GROUPS = [[z * N_Y + y for y in range(N_Y)] for z in range(N_Z)]
PLANES = [[z * N_Y * N_MP + i for i in range(N_Y * N_MP)] for z in range(N_Z)]


def matmul(a, b, dims=NN):
    return lax.dot_general(a, b, dims, precision=HIGH, preferred_element_type=F32)


def places(shape):
    return (
        lax.broadcasted_iota(jnp.int32, shape, 0),
        lax.broadcasted_iota(jnp.int32, shape, 1),
    )


def unit_rows(raw):
    value = raw.astype(F32)
    return value / jnp.sqrt(jnp.sum(value * value, axis=-1, keepdims=True) + EPS)


def invert_all(systems):
    row, col = places((TOK, TOK))
    eye = (row == col).astype(F32)
    close = (row >> 3) == (col >> 3)
    first = [jnp.where(close, low, 0.0) for low in systems]
    second = [matmul(a, a) for a in first]
    fourth = [matmul(a, a) for a in second]
    out = [eye - a for a in first]
    out = [a + matmul(a, b) for a, b in zip(out, second)]
    out = [a + matmul(a, b) for a, b in zip(out, fourth)]
    for shift in (3, 4, 5, 6):
        off = ((row >> (shift + 1)) == (col >> (shift + 1))) & ((row >> shift) != (col >> shift))
        parts = [matmul(jnp.where(off, low, 0.0), a) for low, a in zip(systems, out)]
        out = [a - matmul(a, b) for a, b in zip(out, parts)]
    return out


def small_inputs(dec_ref, beta_ref, rate_ref, bias_ref):
    row, col = places((TOK, TOK))
    falls = []
    for h in range(HEADS):
        pre = dec_ref[h : h + 1, :] + bias_ref[:, h : h + 1]
        soft = jnp.maximum(pre, 0.0) + jnp.log1p(jnp.exp(-jnp.abs(pre)))
        falls.append(-jnp.exp(rate_ref[:, h : h + 1]) * soft)
    cumul = matmul(jnp.concatenate(falls, axis=0), (row <= col).astype(F32))
    return cumul, 1.0 / (1.0 + jnp.exp(-beta_ref[...]))


def delta_parts(cumul, beta, inner, scores):
    row, col = places((TOK, TOK))
    lower = row >= col
    strict = row > col
    mixers, systems, spreads, strengths = [], [], [], []
    for h in range(HEADS):
        wide = jnp.broadcast_to(cumul[h : h + 1, :], (TOK, TOK))
        spread = jnp.where(lower, wide.T - wide, 0.0)
        decay = jnp.where(lower, jnp.exp(spread), 0.0)
        strength = jnp.broadcast_to(beta[h : h + 1, :], (TOK, TOK)).T
        mixers.append(scores * decay)
        systems.append(jnp.where(strict, strength * inner * decay, 0.0))
        spreads.append(spread)
        strengths.append(strength)
    return mixers, systems, spreads, strengths


def forward_kernel(
    k_any, q_any, v_any, up_any, dec_ref, beta_ref, rate_ref, bias_ref, gain_ref,
    g_any, k_ref, q_ref, v_ref, up_ref, g_ref, in_sems, out_sems,
):
    pairs = ((k_any, k_ref), (q_any, q_ref), (v_any, v_ref), (up_any, up_ref))
    fetches = [pltpu.make_async_copy(a, b, in_sems.at[i]) for i, (a, b) in enumerate(pairs)]
    for fetch in fetches:
        fetch.start()
    cumul, beta = small_inputs(dec_ref, beta_ref, rate_ref, bias_ref)
    heads = range(HEADS)
    fetches[0].wait()
    keys = unit_rows(k_ref[...])
    inner = matmul(keys, keys, NT)
    fetches[1].wait()
    scores = matmul(unit_rows(q_ref[...]) * HD ** (-0.5), keys, NT)
    mixers, systems, _, strengths = delta_parts(cumul, beta, inner, scores)
    inverses = invert_all(systems)
    fetches[2].wait()
    scaled = [strengths[h] * v_ref[:, h * HD : (h + 1) * HD].astype(F32) for h in heads]
    writes = [matmul(inverses[h], scaled[h]) for h in heads]
    mixed = [matmul(mixers[h], writes[h]) for h in heads]
    normed = []
    for h in heads:
        scale = lax.rsqrt(jnp.mean(mixed[h] * mixed[h], axis=-1, keepdims=True) + EPS)
        normed.append((mixed[h] * scale * gain_ref[...]).T.astype(BF16))
    left = jnp.concatenate(normed, axis=0)
    fetches[3].wait()
    stores = []
    for z in range(N_Z):
        part = lax.dot_general(
            left, up_ref[:, z * HD : (z + 1) * HD], NN, preferred_element_type=F32
        ).astype(BF16)
        for y in range(N_Y):
            g_ref[z * N_Y + y] = part[y * TILE : (y + 1) * TILE, :]
        tiles = pl.ds(z * N_Y, N_Y)
        stores.append(pltpu.make_async_copy(g_ref.at[tiles], g_any.at[tiles], out_sems.at[z]))
        stores[z].start()
    for store in stores:
        store.wait()


def backward_kernel(
    place_ref, k_any, q_any, v_any, up_any, weight_any, _, dec_ref, beta_ref, rate_ref, bias_ref,
    gain_ref, out_ref, k_ref, q_ref, v_ref, up_ref, weight_ref, in_sems,
):
    pairs = (
        (k_any, k_ref), (q_any, q_ref), (v_any, v_ref), (up_any, up_ref), (weight_any, weight_ref)
    )
    fetches = [pltpu.make_async_copy(a, b, in_sems.at[i]) for i, (a, b) in enumerate(pairs)]
    for fetch in fetches:
        fetch.start()
    for fetch in fetches:
        fetch.wait()
    gain = gain_ref[...]
    d_normed = lax.dot_general(up_ref[...], weight_ref[...], NT, preferred_element_type=F32)
    lane = lax.broadcasted_iota(jnp.int32, (1, HD), 1)
    heads = range(HEADS)
    keys = unit_rows(k_ref[...])
    inner = matmul(keys, keys, NT)
    scores = matmul(unit_rows(q_ref[...]) * HD ** (-0.5), keys, NT)
    cumul, beta = small_inputs(dec_ref, beta_ref, rate_ref, bias_ref)
    mixers, systems, spreads, strengths = delta_parts(cumul, beta, inner, scores)
    inverses = invert_all(systems)
    scaled = [strengths[h] * v_ref[:, h * HD : (h + 1) * HD].astype(F32) for h in heads]
    writes = [matmul(inverses[h], scaled[h]) for h in heads]
    outs = [matmul(mixers[h], writes[h]) for h in heads]
    turns = [matmul(systems[h] * spreads[h], writes[h]) for h in heads]
    turns = [matmul(inverses[h], turns[h]) for h in heads]
    slopes = [
        matmul(mixers[h] * spreads[h], writes[h]) - matmul(mixers[h], turns[h]) for h in heads
    ]
    grad_gain = jnp.zeros((1, HD), F32)
    rates = jnp.zeros((1, HD), F32)
    for h in heads:
        mixed = outs[h]
        scale = lax.rsqrt(jnp.mean(mixed * mixed, axis=-1, keepdims=True) + EPS)
        unit = mixed * scale
        given = d_normed[:, h * HD : (h + 1) * HD]
        grad_gain = grad_gain + jnp.sum(unit * given, axis=0, keepdims=True)
        tilted = given * gain
        d_mixed = scale * (tilted - unit * jnp.mean(unit * tilted, axis=-1, keepdims=True))
        rate = jnp.sum(jnp.sum(d_mixed * slopes[h], axis=0, keepdims=True), axis=1, keepdims=True)
        rates = rates + jnp.where(lane == place_ref[0] * HEADS + h, rate, 0.0)
    out_ref[...] = jnp.concatenate([grad_gain, rates], axis=0)


def gram_kernel(place_ref, x_ref, small_ref, out_ref, wide):
    wide[...] = x_ref[...].astype(F32).reshape(REPS * TILE, HD)
    total = jnp.zeros((REPS, REPS), F32)
    for f in range(0, TILE, 2):
        rows = jnp.concatenate(
            [wide[pl.ds(f + e, REPS, stride=TILE), :].astype(BF16) for e in range(2)], axis=1
        )
        total = total + lax.dot_general(rows, rows, NT, preferred_element_type=F32)
    half = jnp.concatenate([total[: REPS // 2], total[REPS // 2 :]], axis=1)
    fill = jnp.zeros((3, HD), F32)
    for m in range(N_MP):
        kind, y = divmod(m, N_Y)
        extra = jnp.where(place_ref[0] == y, small_ref[kind : kind + 1, :], 0.0)
        block = jnp.concatenate([half[4 * m : 4 * m + 4], extra, fill], axis=0)
        for target in range(N_Y):
            out_ref[target * N_MP + m] = block


def spread_kernel(in_ref, out_ref):
    total = in_ref[0]
    for m in range(1, N_Y * N_MP):
        total = total + in_ref[m]
    out_ref[...] = jnp.broadcast_to(total[None], out_ref.shape)


def gather_kernel(in_ref, out_ref):
    total = in_ref[0, 0:4]
    for z in range(1, N_Z):
        total = total + in_ref[z, 0:4]
    fill = jnp.zeros((4, HD), F32)
    block = jnp.concatenate([total, fill] + [in_ref[z, 4:5] for z in range(N_Z)], axis=0)
    out_ref[...] = jnp.broadcast_to(block[None], out_ref.shape)


def small_tree(stack):
    half = REPS // 2
    while half:
        other = pltpu.roll(stack, half, 0)
        inner = jnp.sum(stack * other, axis=1, keepdims=True)
        norm = jnp.sum(stack * stack, axis=1, keepdims=True)
        part = (1.0 - inner / (2.0 * (norm + EPS))) * stack
        stack = part + pltpu.roll(part, half, 0)
        half //= 2
    return stack[0:1]


def trees_kernel(in_ref, gain_ref, rate_ref):
    for kind, out in enumerate((gain_ref, rate_ref)):
        rows = [in_ref[kind * N_Y + r % N_Y, 8 + r // N_Y : 9 + r // N_Y, :] for r in range(REPS)]
        out[...] = small_tree(jnp.concatenate(rows, axis=0))


def path_coefs(gram):
    row, lane = places((REPS, HD))
    same = row == (lane & (REPS - 1))
    near = row == lane
    coefs = jnp.ones((REPS, 1), F32)
    half = REPS // 2
    while half:
        other = pltpu.roll(gram, half, 1)
        norm_col = jnp.sum(jnp.where(near, gram, 0.0), axis=1, keepdims=True)
        inner_col = jnp.sum(jnp.where(near, other, 0.0), axis=1, keepdims=True)
        norm_row = jnp.sum(jnp.where(same, gram, 0.0), axis=0, keepdims=True)
        inner_row = jnp.sum(jnp.where(same, other, 0.0), axis=0, keepdims=True)
        by_col = 1.0 - inner_col / (2.0 * (norm_col + EPS))
        by_row = 1.0 - inner_row / (2.0 * (norm_row + EPS))
        coefs = coefs * by_col
        part = by_col * by_row * gram
        part = part + pltpu.roll(part, half, 1)
        gram = part + pltpu.roll(part, half, 0)
        half //= 2
    return coefs


def combine_kernel(gram_ref, x_ref, out_ref, factor):
    lane = lax.broadcasted_iota(jnp.int32, (REPS // 2, HD), 1)
    packed = jnp.concatenate([gram_ref[m, 0:4] for m in range(N_MP)], axis=0)
    turned = pltpu.roll(packed, REPS, 1)
    gram = jnp.concatenate(
        [jnp.where(lane < REPS, packed, turned), jnp.where(lane < REPS, turned, packed)], axis=0
    )
    factor[...] = jnp.broadcast_to(path_coefs(gram), (REPS, HD))
    total = jnp.zeros((TILE, HD), F32)
    for r in range(REPS):
        total = total + factor[r : r + 1, :] * x_ref[r].astype(F32)
    out_ref[...] = jnp.broadcast_to(total.astype(BF16)[None], out_ref.shape)


def unfold_kernel(in_ref, out_ref):
    for z in range(N_Z):
        out_ref[:, :, z * HD : (z + 1) * HD] = jnp.broadcast_to(
            in_ref[z][None], (N_Y, TILE, HD)
        )


def call(body, outs, ops, scratch=(), smem=(), hbm=(), out_hbm=(), flops=0, limit=LIMIT):
    size = sum(o.size * o.dtype.itemsize for o in ops) + sum(o.size * o.dtype.itemsize for o in outs)
    spaces = [
        pltpu.SMEM if i in smem else pl.ANY if i in hbm else pltpu.VMEM for i in range(len(ops))
    ]
    return pl.pallas_call(
        body,
        out_shape=outs,
        in_specs=[pl.BlockSpec(memory_space=space) for space in spaces],
        out_specs=[
            pl.BlockSpec(memory_space=pl.ANY if i in out_hbm else pltpu.VMEM)
            for i in range(len(outs))
        ],
        scratch_shapes=list(scratch),
        compiler_params=pltpu.CompilerParams(vmem_limit_bytes=limit),
        cost_estimate=pl.CostEstimate(flops=flops, bytes_accessed=size, transcendentals=0),
    )(*ops)


def shape(dims, dtype=F32):
    return jax.ShapeDtypeStruct(dims, dtype)


def forward(big, rows, gain_row):
    (tiles,) = call(
        forward_kernel,
        [shape((REPS, TILE, HD), BF16)],
        [*big, *rows, gain_row],
        scratch=[pltpu.VMEM(a.shape, BF16) for a in big]
        + [
            pltpu.VMEM((REPS, TILE, HD), BF16),
            pltpu.SemaphoreType.DMA((4,)),
            pltpu.SemaphoreType.DMA((N_Z,)),
        ],
        hbm=(0, 1, 2, 3),
        out_hbm=(0,),
        limit=56 * 2**20,
        flops=2 * 10**9,
    )
    return tiles


def backward(place, big, tiles, rows, gain_row):
    (small,) = call(
        backward_kernel,
        [shape((2, HD))],
        [place, *big, tiles, *rows, gain_row],
        scratch=[pltpu.VMEM(a.shape, BF16) for a in big] + [pltpu.SemaphoreType.DMA((5,))],
        smem=(0,),
        hbm=(1, 2, 3, 4, 5, 6),
        limit=56 * 2**20,
        flops=2 * 10**9,
    )
    return small


def gram(stack, small, place):
    (part,) = call(
        gram_kernel,
        [shape((N_Y * N_MP, 8, HD))],
        [place, stack, small],
        scratch=[pltpu.VMEM((REPS * TILE, HD), F32)],
        smem=(0,),
        flops=10**9,
    )
    return part


def combine(packed, stack):
    (tile,) = call(
        combine_kernel,
        [shape((N_Z, TILE, HD), BF16)],
        [packed, stack],
        scratch=[pltpu.VMEM((REPS, HD), F32)],
        flops=10**8,
    )
    return tile


def per_device(
    query_raw, key_raw, values, decay_input, beta_input, log_rate, step_bias, gain, out_weight, upstream
):
    gain_row = gain[None, :]
    big = (key_raw, query_raw, values, upstream)
    rows = (decay_input.T, beta_input.T, log_rate[None, :], step_bias[None, :])
    tiles = forward(big, rows, gain_row)
    stack = lax.all_to_all(tiles, "dp", 0, 0)
    place = lax.axis_index("mp").astype(jnp.int32)[None]
    small = backward(place, (*big, out_weight), tiles, rows, gain_row)
    place = (lax.axis_index("dp") % N_Y).astype(jnp.int32)[None]
    part = gram(stack, small, place)
    part = lax.all_to_all(part, ("dp", "mp"), 0, 0, axis_index_groups=PLANES)
    (part,) = call(spread_kernel, [shape((N_Z, 8, HD))], [part])
    part = lax.all_to_all(part, "dp", 0, 0, axis_index_groups=Z_GROUPS)
    (part,) = call(gather_kernel, [shape((N_MP, 24, HD))], [part])
    packed = lax.all_to_all(part, "mp", 0, 0)
    whole = combine(packed, stack)
    whole = lax.all_to_all(whole, "dp", 0, 0, axis_index_groups=Z_GROUPS)
    (whole,) = call(unfold_kernel, [shape((N_Y, TILE, N_Z * HD), BF16)], [whole])
    whole = lax.all_to_all(whole, "dp", 0, 0, axis_index_groups=Y_GROUPS)
    gain_final, rate_final = call(trees_kernel, [shape((1, HD)), shape((1, HD))], [packed])
    return (
        whole.reshape(N_Y * TILE, N_Z * HD),
        gain_final[0],
        rate_final[0, : HEADS * N_MP],
    )


def solution(mesh):
    in_specs = (
        P("dp", "mp"),
        P("dp", "mp"),
        P("dp", "mp"),
        P("dp", "mp"),
        P("dp", "mp"),
        P("mp"),
        P("mp"),
        P(),
        P("mp", None),
        P("dp", None),
    )
    out_specs = (P("mp", None), P(), P())
    return jax.shard_map(
        per_device, mesh=mesh, in_specs=in_specs, out_specs=out_specs, check_vma=False
    )
```

```python
import functools

import jax
import jax.numpy as jnp
from jax import lax
from jax.experimental import pallas as pl
from jax.experimental.pallas import tpu as pltpu
from jax.sharding import PartitionSpec as P

EPS = 1e-06
F32 = jnp.float32
BF16 = jnp.bfloat16
HIGH = lax.Precision.HIGHEST
TOK = 128
HD = 128
HEADS = 2
REPS = 64
N_Z = 16
N_Y = 4
N_MP = 8
TILE = 64
LIMIT = 48 * 1024 * 1024
NN = (((1,), (0,)), ((), ()))
NT = (((1,), (1,)), ((), ()))

Z_GROUPS = [[z * N_Y + y for z in range(N_Z)] for y in range(N_Y)]
Y_GROUPS = [[z * N_Y + y for y in range(N_Y)] for z in range(N_Z)]
PLANES = [[z * N_Y * N_MP + i for i in range(N_Y * N_MP)] for z in range(N_Z)]


def matmul(a, b, dims=NN):
    return lax.dot_general(a, b, dims, precision=HIGH, preferred_element_type=F32)


def places(shape):
    return (
        lax.broadcasted_iota(jnp.int32, shape, 0),
        lax.broadcasted_iota(jnp.int32, shape, 1),
    )


def unit_rows(raw):
    value = raw.astype(F32)
    return value / jnp.sqrt(jnp.sum(value * value, axis=-1, keepdims=True) + EPS)


def within(shift):
    row, col = places((TOK, TOK))
    return (row >> shift) == (col >> shift)


def invert_blocks(systems):
    eye = within(0).astype(F32)
    first = [jnp.where(within(3), low, 0.0) for low in systems]
    second = [matmul(a, a) for a in first]
    out = [eye - a for a in first]
    fourth = [matmul(a, a) for a in second]
    out = [a + matmul(a, b) for a, b in zip(out, second)]
    return [a + matmul(a, b) for a, b in zip(out, fourth)]


def widen(systems, inverses, given, shift):
    rest = within(shift + 2) & ~within(shift)
    steps = [matmul(a, jnp.where(rest, low, 0.0)) for low, a in zip(systems, inverses)]
    out = inverses if given is None else [matmul(a, v) for a, v in zip(inverses, given)]
    squares = [matmul(a, a) for a in steps]
    out = [v - matmul(a, v) for a, v in zip(steps, out)]
    return [v + matmul(a, v) for a, v in zip(squares, out)]


def solve_all(systems, given):
    inverses = widen(systems, invert_blocks(systems), None, 3)
    return widen(systems, inverses, given, 5)


def small_inputs(dec_ref, beta_ref, rate_ref, bias_ref):
    row, col = places((TOK, TOK))
    falls = []
    for h in range(HEADS):
        pre = dec_ref[h : h + 1, :] + bias_ref[:, h : h + 1]
        soft = jnp.maximum(pre, 0.0) + jnp.log1p(jnp.exp(-jnp.abs(pre)))
        falls.append(-jnp.exp(rate_ref[:, h : h + 1]) * soft)
    cumul = matmul(jnp.concatenate(falls, axis=0), (row <= col).astype(F32))
    return cumul, 1.0 / (1.0 + jnp.exp(-beta_ref[...]))


def delta_parts(cumul, beta, inner, scores):
    row, col = places((TOK, TOK))
    lower = row >= col
    strict = row > col
    mixers, systems, spreads, strengths = [], [], [], []
    for h in range(HEADS):
        wide = jnp.broadcast_to(cumul[h : h + 1, :], (TOK, TOK))
        spread = jnp.where(lower, wide.T - wide, 0.0)
        decay = jnp.where(lower, jnp.exp(spread), 0.0)
        strength = jnp.broadcast_to(beta[h : h + 1, :], (TOK, TOK)).T
        mixers.append(scores * decay)
        systems.append(jnp.where(strict, strength * inner * decay, 0.0))
        spreads.append(spread)
        strengths.append(strength)
    return mixers, systems, spreads, strengths


def forward_kernel(
    k_any, q_any, v_any, up_any, dec_ref, beta_ref, rate_ref, bias_ref, gain_ref,
    g_any, k_ref, q_ref, v_ref, up_ref, g_ref, in_sems, out_sems,
):
    pairs = ((k_any, k_ref), (q_any, q_ref), (v_any, v_ref), (up_any, up_ref))
    fetches = [pltpu.make_async_copy(a, b, in_sems.at[i]) for i, (a, b) in enumerate(pairs)]
    for fetch in fetches:
        fetch.start()
    cumul, beta = small_inputs(dec_ref, beta_ref, rate_ref, bias_ref)
    heads = range(HEADS)
    fetches[0].wait()
    keys = unit_rows(k_ref[...])
    inner = matmul(keys, keys, NT)
    fetches[1].wait()
    scores = matmul(unit_rows(q_ref[...]) * HD ** (-0.5), keys, NT)
    mixers, systems, _, strengths = delta_parts(cumul, beta, inner, scores)
    fetches[2].wait()
    scaled = [strengths[h] * v_ref[:, h * HD : (h + 1) * HD].astype(F32) for h in heads]
    writes = solve_all(systems, scaled)
    mixed = [matmul(mixers[h], writes[h]) for h in heads]
    normed = []
    for h in heads:
        scale = lax.rsqrt(jnp.mean(mixed[h] * mixed[h], axis=-1, keepdims=True) + EPS)
        normed.append((mixed[h] * scale * gain_ref[...]).T.astype(BF16))
    left = jnp.concatenate(normed, axis=0)
    fetches[3].wait()
    stores = []
    for z in range(N_Z):
        part = lax.dot_general(
            left, up_ref[:, z * HD : (z + 1) * HD], NN, preferred_element_type=F32
        ).astype(BF16)
        for y in range(N_Y):
            g_ref[z * N_Y + y] = part[y * TILE : (y + 1) * TILE, :]
        tiles = pl.ds(z * N_Y, N_Y)
        stores.append(pltpu.make_async_copy(g_ref.at[tiles], g_any.at[tiles], out_sems.at[z]))
        stores[z].start()
    for store in stores:
        store.wait()


def backward_kernel(
    place_ref, k_any, q_any, v_any, up_any, weight_any, _, dec_ref, beta_ref, rate_ref, bias_ref,
    gain_ref, out_ref, k_ref, q_ref, v_ref, up_ref, weight_ref, in_sems,
):
    pairs = (
        (k_any, k_ref), (q_any, q_ref), (v_any, v_ref), (up_any, up_ref), (weight_any, weight_ref)
    )
    fetches = [pltpu.make_async_copy(a, b, in_sems.at[i]) for i, (a, b) in enumerate(pairs)]
    for fetch in fetches:
        fetch.start()
    for fetch in fetches:
        fetch.wait()
    gain = gain_ref[...]
    d_normed = lax.dot_general(up_ref[...], weight_ref[...], NT, preferred_element_type=F32)
    lane = lax.broadcasted_iota(jnp.int32, (1, HD), 1)
    heads = range(HEADS)
    keys = unit_rows(k_ref[...])
    inner = matmul(keys, keys, NT)
    scores = matmul(unit_rows(q_ref[...]) * HD ** (-0.5), keys, NT)
    cumul, beta = small_inputs(dec_ref, beta_ref, rate_ref, bias_ref)
    mixers, systems, spreads, strengths = delta_parts(cumul, beta, inner, scores)
    scaled = [strengths[h] * v_ref[:, h * HD : (h + 1) * HD].astype(F32) for h in heads]
    writes = solve_all(systems, scaled)
    outs = [matmul(mixers[h], writes[h]) for h in heads]
    turns = solve_all(systems, [matmul(systems[h] * spreads[h], writes[h]) for h in heads])
    slopes = [
        matmul(mixers[h] * spreads[h], writes[h]) - matmul(mixers[h], turns[h]) for h in heads
    ]
    grad_gain = jnp.zeros((1, HD), F32)
    rates = jnp.zeros((1, HD), F32)
    for h in heads:
        mixed = outs[h]
        scale = lax.rsqrt(jnp.mean(mixed * mixed, axis=-1, keepdims=True) + EPS)
        unit = mixed * scale
        given = d_normed[:, h * HD : (h + 1) * HD]
        grad_gain = grad_gain + jnp.sum(unit * given, axis=0, keepdims=True)
        tilted = given * gain
        d_mixed = scale * (tilted - unit * jnp.mean(unit * tilted, axis=-1, keepdims=True))
        rate = jnp.sum(jnp.sum(d_mixed * slopes[h], axis=0, keepdims=True), axis=1, keepdims=True)
        rates = rates + jnp.where(lane == place_ref[0] * HEADS + h, rate, 0.0)
    out_ref[...] = jnp.concatenate([grad_gain, rates], axis=0)


def turn_rows(value, sign):
    row, _ = places(value.shape)
    parts = []
    for g in range(REPS // 8):
        part = value[8 * g : 8 * g + 8]
        parts.append(pltpu.roll(part, (sign * 8 * g) % HD, 1) if g else part)
    value = jnp.concatenate(parts, axis=0)
    for bit in range(3):
        value = jnp.where(
            (row >> bit) & 1 == 1, pltpu.roll(value, (sign * 2**bit) % HD, 1), value
        )
    return value


def twice(value):
    return jnp.concatenate([value, value], axis=1)


def pack_gram(total):
    row, lane = places((REPS, HD))
    wide = twice(total)
    turned = turn_rows(wide, -1)
    _, slot = places((16, HD))
    packed = turned[0:16]
    for q in range(1, 4):
        packed = jnp.where(
            slot >> 5 == q, pltpu.roll(turned[16 * q : 16 * q + 16], 32 * q, 1), packed
        )
    across = jnp.where(lane < REPS, (lane + 32) & (REPS - 1), lane - REPS)
    return packed, jnp.sum(jnp.where(row == across, wide, 0.0), axis=0, keepdims=True)


def unpack_gram(packed, last):
    row, lane = places((REPS, HD))
    turned = jnp.concatenate(
        [packed] + [pltpu.roll(packed, HD - 32 * q, 1) for q in range(1, 4)], axis=0
    )
    upper = turn_rows(jnp.where(lane < 32, turned, 0.0), 1)
    upper = upper + pltpu.roll(upper, REPS, 1)
    col = lane & (REPS - 1)
    other = jnp.where(row == col, 0.0, twice(upper[:, :REPS].T))
    turned = pltpu.roll(last, REPS, 1)
    half = jnp.where(lane[0:1] < REPS, last, turned)
    rest = jnp.where(lane[0:1] < REPS, turned, last)
    half = jnp.where(row == (col + 32) & (REPS - 1), half, 0.0)
    return upper + other + half + jnp.where(row == col, rest, 0.0)


def gram_kernel(place_ref, x_ref, small_ref, out_ref, wide):
    wide[...] = x_ref[...].astype(F32).reshape(REPS * TILE, HD)
    total = jnp.zeros((REPS, REPS), F32)
    for f in range(0, TILE, 2):
        rows = jnp.concatenate(
            [wide[pl.ds(f + e, REPS, stride=TILE), :].astype(BF16) for e in range(2)], axis=1
        )
        total = total + lax.dot_general(rows, rows, NT, preferred_element_type=F32)
    packed, last = pack_gram(total)
    gain, rate = small_ref[0:1, :], small_ref[1:2, :]
    own = [place_ref[0] == y for y in range(N_Y)]
    rates = jnp.where(own[0], rate, 0.0)
    for y in range(1, N_Y):
        rates = jnp.where(own[y], pltpu.roll(rate, 16 * y, 1), rates)
    gains = [jnp.where(own[y], gain, 0.0) for y in range(N_Y)]
    block = jnp.concatenate([packed, last, rates, *gains, jnp.zeros((2, HD), F32)], axis=0)
    out_ref[...] = jnp.broadcast_to(block[None], out_ref.shape)


def split(value):
    high = value.astype(BF16).astype(F32)
    return high, value - high


def spread_kernel(in_ref, out_ref):
    total = in_ref[0]
    for m in range(1, N_Y * N_MP):
        total = total + in_ref[m]
    high, low = split(total)
    lane = lax.broadcasted_iota(jnp.int32, (1, HD), 1)
    last = jnp.where(lane < REPS, high[16:17], low[16:17])
    rates = jnp.where(lane < REPS, high[17:18], pltpu.roll(low[17:18], REPS, 1))
    block = jnp.concatenate(
        [high[0:16], last, rates, high[18:22], low[18:22], jnp.zeros((6, HD), F32)], axis=0
    )
    out_ref[...] = jnp.broadcast_to(block.astype(BF16)[None], out_ref.shape)


def small_tree(stack):
    half = REPS // 2
    while half:
        other = pltpu.roll(stack, half, 0)
        inner = jnp.sum(stack * other, axis=1, keepdims=True)
        norm = jnp.sum(stack * stack, axis=1, keepdims=True)
        part = (1.0 - inner / (2.0 * (norm + EPS))) * stack
        stack = part + pltpu.roll(part, half, 0)
        half //= 2
    return stack[0:1]


def trees_kernel(in_ref, gain_ref, rate_ref):
    lane = lax.broadcasted_iota(jnp.int32, (1, HD), 1)
    gains, rates = [], []
    for z in range(N_Z):
        block = in_ref[z].astype(F32)
        gains.append(block[18:22] + block[22:26])
        row = block[17:18]
        row = row + pltpu.roll(row, REPS, 1)
        for y in range(N_Y):
            rates.append(jnp.where(lane < 16, pltpu.roll(row, (-16 * y) % HD, 1), 0.0))
    gain_ref[...] = small_tree(jnp.concatenate(gains, axis=0))
    rate_ref[...] = small_tree(jnp.concatenate(rates, axis=0))


def path_coefs(gram):
    row, lane = places((REPS, HD))
    same = row == (lane & (REPS - 1))
    near = row == lane
    coefs = jnp.ones((REPS, 1), F32)
    half = REPS // 2
    while half:
        other = pltpu.roll(gram, half, 1)
        norm_col = jnp.sum(jnp.where(near, gram, 0.0), axis=1, keepdims=True)
        inner_col = jnp.sum(jnp.where(near, other, 0.0), axis=1, keepdims=True)
        norm_row = jnp.sum(jnp.where(same, gram, 0.0), axis=0, keepdims=True)
        inner_row = jnp.sum(jnp.where(same, other, 0.0), axis=0, keepdims=True)
        by_col = 1.0 - inner_col / (2.0 * (norm_col + EPS))
        by_row = 1.0 - inner_row / (2.0 * (norm_row + EPS))
        coefs = coefs * by_col
        part = by_col * by_row * gram
        part = part + pltpu.roll(part, half, 1)
        gram = part + pltpu.roll(part, half, 0)
        half //= 2
    return coefs


def combine_kernel(in_ref, x_ref, out_ref, factor):
    total = in_ref[0].astype(F32)
    for z in range(1, N_Z):
        total = total + in_ref[z].astype(F32)
    gram = unpack_gram(total[0:16], total[16:17])
    factor[...] = jnp.broadcast_to(path_coefs(gram), (REPS, HD))
    total = jnp.zeros((TILE, HD), F32)
    for r in range(REPS):
        total = total + factor[r : r + 1, :] * x_ref[r].astype(F32)
    out_ref[...] = jnp.broadcast_to(total.astype(BF16)[None], out_ref.shape)


def unfold_kernel(in_ref, out_ref):
    for z in range(N_Z):
        out_ref[:, :, z * HD : (z + 1) * HD] = jnp.broadcast_to(
            in_ref[z][None], (N_Y, TILE, HD)
        )


def call(body, outs, ops, scratch=(), smem=(), hbm=(), out_hbm=(), flops=0, limit=LIMIT):
    size = sum(o.size * o.dtype.itemsize for o in ops) + sum(o.size * o.dtype.itemsize for o in outs)
    spaces = [
        pltpu.SMEM if i in smem else pl.ANY if i in hbm else pltpu.VMEM for i in range(len(ops))
    ]
    return pl.pallas_call(
        body,
        out_shape=outs,
        in_specs=[pl.BlockSpec(memory_space=space) for space in spaces],
        out_specs=[
            pl.BlockSpec(memory_space=pl.ANY if i in out_hbm else pltpu.VMEM)
            for i in range(len(outs))
        ],
        scratch_shapes=list(scratch),
        compiler_params=pltpu.CompilerParams(vmem_limit_bytes=limit),
        cost_estimate=pl.CostEstimate(flops=flops, bytes_accessed=size, transcendentals=0),
    )(*ops)


def shape(dims, dtype=F32):
    return jax.ShapeDtypeStruct(dims, dtype)


def forward(big, rows, gain_row):
    (tiles,) = call(
        forward_kernel,
        [shape((REPS, TILE, HD), BF16)],
        [*big, *rows, gain_row],
        scratch=[pltpu.VMEM(a.shape, BF16) for a in big]
        + [
            pltpu.VMEM((REPS, TILE, HD), BF16),
            pltpu.SemaphoreType.DMA((4,)),
            pltpu.SemaphoreType.DMA((N_Z,)),
        ],
        hbm=(0, 1, 2, 3),
        out_hbm=(0,),
        limit=56 * 2**20,
        flops=2 * 10**9,
    )
    return tiles


def backward(place, big, tiles, rows, gain_row):
    (small,) = call(
        backward_kernel,
        [shape((2, HD))],
        [place, *big, tiles, *rows, gain_row],
        scratch=[pltpu.VMEM(a.shape, BF16) for a in big] + [pltpu.SemaphoreType.DMA((5,))],
        smem=(0,),
        hbm=(1, 2, 3, 4, 5, 6),
        limit=56 * 2**20,
        flops=2 * 10**9,
    )
    return small


def gram(stack, small, place):
    (part,) = call(
        gram_kernel,
        [shape((N_Y * N_MP, 24, HD))],
        [place, stack, small],
        scratch=[pltpu.VMEM((REPS * TILE, HD), F32)],
        smem=(0,),
        flops=10**9,
    )
    return part


def combine(packed, stack):
    (tile,) = call(
        combine_kernel,
        [shape((N_Z, TILE, HD), BF16)],
        [packed, stack],
        scratch=[pltpu.VMEM((REPS, HD), F32)],
        flops=10**8,
    )
    return tile


def per_device(
    query_raw, key_raw, values, decay_input, beta_input, log_rate, step_bias, gain, out_weight, upstream
):
    gain_row = gain[None, :]
    big = (key_raw, query_raw, values, upstream)
    rows = (decay_input.T, beta_input.T, log_rate[None, :], step_bias[None, :])
    tiles = forward(big, rows, gain_row)
    stack = lax.all_to_all(tiles, "dp", 0, 0)
    place = lax.axis_index("mp").astype(jnp.int32)[None]
    small = backward(place, (*big, out_weight), tiles, rows, gain_row)
    place = (lax.axis_index("dp") % N_Y).astype(jnp.int32)[None]
    part = gram(stack, small, place)
    part = lax.all_to_all(part, ("dp", "mp"), 0, 0, axis_index_groups=PLANES)
    (part,) = call(spread_kernel, [shape((N_Z, 32, HD), BF16)], [part])
    packed = lax.all_to_all(part, "dp", 0, 0, axis_index_groups=Z_GROUPS)
    whole = combine(packed, stack)
    whole = lax.all_to_all(whole, "dp", 0, 0, axis_index_groups=Z_GROUPS)
    (whole,) = call(unfold_kernel, [shape((N_Y, TILE, N_Z * HD), BF16)], [whole])
    whole = lax.all_to_all(whole, "dp", 0, 0, axis_index_groups=Y_GROUPS)
    gain_final, rate_final = call(trees_kernel, [shape((1, HD)), shape((1, HD))], [packed])
    return (
        whole.reshape(N_Y * TILE, N_Z * HD),
        gain_final[0],
        rate_final[0, : HEADS * N_MP],
    )


def solution(mesh):
    in_specs = (
        P("dp", "mp"),
        P("dp", "mp"),
        P("dp", "mp"),
        P("dp", "mp"),
        P("dp", "mp"),
        P("mp"),
        P("mp"),
        P(),
        P("mp", None),
        P("dp", None),
    )
    out_specs = (P("mp", None), P(), P())
    return jax.shard_map(
        per_device, mesh=mesh, in_specs=in_specs, out_specs=out_specs, check_vma=False
    )
```

```python
import functools

import jax
import jax.numpy as jnp
from jax import lax
from jax.experimental import pallas as pl
from jax.experimental.pallas import tpu as pltpu
from jax.sharding import PartitionSpec as P

EPS = 1e-06
F32 = jnp.float32
BF16 = jnp.bfloat16
HIGH = lax.Precision.HIGHEST
TOK = 128
HD = 128
HEADS = 2
REPS = 64
N_Z = 16
N_Y = 4
N_MP = 8
TILE = 64
LIMIT = 48 * 1024 * 1024
NN = (((1,), (0,)), ((), ()))
NT = (((1,), (1,)), ((), ()))

Z_GROUPS = [[z * N_Y + y for z in range(N_Z)] for y in range(N_Y)]
Y_GROUPS = [[z * N_Y + y for y in range(N_Y)] for z in range(N_Z)]
PLANES = [[z * N_Y * N_MP + i for i in range(N_Y * N_MP)] for z in range(N_Z)]


def matmul(a, b, dims=NN):
    return lax.dot_general(a, b, dims, precision=HIGH, preferred_element_type=F32)


def matmul3(a, b, dims=NN):
    ah, bh = a.astype(BF16), b.astype(BF16)
    al, bl = (a - ah.astype(F32)).astype(BF16), (b - bh.astype(F32)).astype(BF16)
    dot = functools.partial(lax.dot_general, dimension_numbers=dims, preferred_element_type=F32)
    return dot(ah, bh) + (dot(ah, bl) + dot(al, bh))


def places(shape):
    return (
        lax.broadcasted_iota(jnp.int32, shape, 0),
        lax.broadcasted_iota(jnp.int32, shape, 1),
    )


def unit_rows(raw):
    value = raw.astype(F32)
    return value / jnp.sqrt(jnp.sum(value * value, axis=-1, keepdims=True) + EPS)


def within(shift):
    row, col = places((TOK, TOK))
    return (row >> shift) == (col >> shift)


def invert_blocks(systems, mul):
    eye = within(0).astype(F32)
    first = [jnp.where(within(3), low, 0.0) for low in systems]
    second = [mul(a, a) for a in first]
    out = [eye - a for a in first]
    fourth = [mul(a, a) for a in second]
    out = [a + mul(a, b) for a, b in zip(out, second)]
    return [a + mul(a, b) for a, b in zip(out, fourth)]


def widen(systems, inverses, given, shift, mul):
    rest = within(shift + 2) & ~within(shift)
    steps = [mul(a, jnp.where(rest, low, 0.0)) for low, a in zip(systems, inverses)]
    out = inverses if given is None else [mul(a, v) for a, v in zip(inverses, given)]
    squares = [mul(a, a) for a in steps]
    out = [v - mul(a, v) for a, v in zip(steps, out)]
    return [v + mul(a, v) for a, v in zip(squares, out)]


def solve_all(systems, given, mul=matmul):
    inverses = widen(systems, invert_blocks(systems, mul), None, 3, mul)
    return widen(systems, inverses, given, 5, mul)


def small_inputs(dec_ref, beta_ref, rate_ref, bias_ref):
    row, col = places((TOK, TOK))
    falls = []
    for h in range(HEADS):
        pre = dec_ref[h : h + 1, :] + bias_ref[:, h : h + 1]
        soft = jnp.maximum(pre, 0.0) + jnp.log1p(jnp.exp(-jnp.abs(pre)))
        falls.append(-jnp.exp(rate_ref[:, h : h + 1]) * soft)
    cumul = matmul(jnp.concatenate(falls, axis=0), (row <= col).astype(F32))
    return cumul, 1.0 / (1.0 + jnp.exp(-beta_ref[...]))


def delta_parts(cumul, beta, inner, scores):
    row, col = places((TOK, TOK))
    lower = row >= col
    strict = row > col
    mixers, systems, spreads, strengths = [], [], [], []
    for h in range(HEADS):
        wide = jnp.broadcast_to(cumul[h : h + 1, :], (TOK, TOK))
        spread = jnp.where(lower, wide.T - wide, 0.0)
        decay = jnp.where(lower, jnp.exp(spread), 0.0)
        strength = jnp.broadcast_to(beta[h : h + 1, :], (TOK, TOK)).T
        mixers.append(scores * decay)
        systems.append(jnp.where(strict, strength * inner * decay, 0.0))
        spreads.append(spread)
        strengths.append(strength)
    return mixers, systems, spreads, strengths


def forward_kernel(
    k_any, q_any, v_any, up_any, dec_ref, beta_ref, rate_ref, bias_ref, gain_ref,
    g_any, k_ref, q_ref, v_ref, up_ref, g_ref, in_sems, out_sems,
):
    pairs = ((k_any, k_ref), (q_any, q_ref), (v_any, v_ref), (up_any, up_ref))
    fetches = [pltpu.make_async_copy(a, b, in_sems.at[i]) for i, (a, b) in enumerate(pairs)]
    for fetch in fetches:
        fetch.start()
    cumul, beta = small_inputs(dec_ref, beta_ref, rate_ref, bias_ref)
    heads = range(HEADS)
    fetches[0].wait()
    keys = unit_rows(k_ref[...])
    inner = matmul3(keys, keys, NT)
    fetches[1].wait()
    scores = matmul3(unit_rows(q_ref[...]) * HD ** (-0.5), keys, NT)
    mixers, systems, _, strengths = delta_parts(cumul, beta, inner, scores)
    fetches[2].wait()
    scaled = [strengths[h] * v_ref[:, h * HD : (h + 1) * HD].astype(F32) for h in heads]
    writes = solve_all(systems, scaled, matmul3)
    mixed = [matmul3(mixers[h], writes[h]) for h in heads]
    normed = []
    for h in heads:
        scale = lax.rsqrt(jnp.mean(mixed[h] * mixed[h], axis=-1, keepdims=True) + EPS)
        normed.append((mixed[h] * scale * gain_ref[...]).T.astype(BF16))
    left = jnp.concatenate(normed, axis=0)
    fetches[3].wait()
    stores = []
    for z in range(N_Z):
        part = lax.dot_general(
            left, up_ref[:, z * HD : (z + 1) * HD], NN, preferred_element_type=F32
        ).astype(BF16)
        for y in range(N_Y):
            g_ref[z * N_Y + y] = part[y * TILE : (y + 1) * TILE, :]
        tiles = pl.ds(z * N_Y, N_Y)
        stores.append(pltpu.make_async_copy(g_ref.at[tiles], g_any.at[tiles], out_sems.at[z]))
        stores[z].start()
    for store in stores:
        store.wait()


def backward_kernel(
    place_ref, k_any, q_any, v_any, up_any, weight_any, _, dec_ref, beta_ref, rate_ref, bias_ref,
    gain_ref, out_ref, k_ref, q_ref, v_ref, up_ref, weight_ref, in_sems,
):
    pairs = (
        (k_any, k_ref), (q_any, q_ref), (v_any, v_ref), (up_any, up_ref), (weight_any, weight_ref)
    )
    fetches = [pltpu.make_async_copy(a, b, in_sems.at[i]) for i, (a, b) in enumerate(pairs)]
    for fetch in fetches:
        fetch.start()
    for fetch in fetches:
        fetch.wait()
    gain = gain_ref[...]
    d_normed = lax.dot_general(up_ref[...], weight_ref[...], NT, preferred_element_type=F32)
    lane = lax.broadcasted_iota(jnp.int32, (1, HD), 1)
    heads = range(HEADS)
    keys = unit_rows(k_ref[...])
    inner = matmul(keys, keys, NT)
    scores = matmul(unit_rows(q_ref[...]) * HD ** (-0.5), keys, NT)
    cumul, beta = small_inputs(dec_ref, beta_ref, rate_ref, bias_ref)
    mixers, systems, spreads, strengths = delta_parts(cumul, beta, inner, scores)
    scaled = [strengths[h] * v_ref[:, h * HD : (h + 1) * HD].astype(F32) for h in heads]
    writes = solve_all(systems, scaled)
    outs = [matmul(mixers[h], writes[h]) for h in heads]
    turns = solve_all(systems, [matmul(systems[h] * spreads[h], writes[h]) for h in heads])
    slopes = [
        matmul(mixers[h] * spreads[h], writes[h]) - matmul(mixers[h], turns[h]) for h in heads
    ]
    grad_gain = jnp.zeros((1, HD), F32)
    rates = jnp.zeros((1, HD), F32)
    for h in heads:
        mixed = outs[h]
        scale = lax.rsqrt(jnp.mean(mixed * mixed, axis=-1, keepdims=True) + EPS)
        unit = mixed * scale
        given = d_normed[:, h * HD : (h + 1) * HD]
        grad_gain = grad_gain + jnp.sum(unit * given, axis=0, keepdims=True)
        tilted = given * gain
        d_mixed = scale * (tilted - unit * jnp.mean(unit * tilted, axis=-1, keepdims=True))
        rate = jnp.sum(jnp.sum(d_mixed * slopes[h], axis=0, keepdims=True), axis=1, keepdims=True)
        rates = rates + jnp.where(lane == place_ref[0] * HEADS + h, rate, 0.0)
    out_ref[...] = jnp.concatenate([grad_gain, rates], axis=0)


def turn_left(value):
    row, _ = places(value.shape)
    parts = []
    for g in range(REPS // 8):
        part = value[8 * g : 8 * g + 8]
        parts.append(pltpu.roll(part, HD - 8 * g, 1) if g else part)
    value = jnp.concatenate(parts, axis=0)
    for bit in range(3):
        value = jnp.where((row >> bit) & 1 == 1, pltpu.roll(value, HD - 2**bit, 1), value)
    return value


def turn_right(value):
    parts = [
        pltpu.roll(value[8 * g : 8 * g + 8], 8 * g, 1, stride=1, stride_axis=0)
        for g in range(REPS // 8)
    ]
    return jnp.concatenate(parts, axis=0)


def twice(value):
    return jnp.concatenate([value, value], axis=1)


def pack_gram(total):
    row, lane = places((REPS, HD))
    wide = twice(total)
    turned = turn_left(wide)
    _, slot = places((16, HD))
    packed = turned[0:16]
    for q in range(1, 4):
        packed = jnp.where(
            slot >> 5 == q, pltpu.roll(turned[16 * q : 16 * q + 16], 32 * q, 1), packed
        )
    across = (lane < REPS) & (row == (lane + 32) & (REPS - 1))
    return packed, jnp.sum(jnp.where(across, wide, 0.0), axis=0, keepdims=True)


def unpack_gram(packed, last):
    row, lane = places((REPS, HD))
    turned = jnp.concatenate(
        [packed] + [pltpu.roll(packed, HD - 32 * q, 1) for q in range(1, 4)], axis=0
    )
    upper = turn_right(jnp.where(lane < 32, turned, 0.0))
    upper = upper + pltpu.roll(upper, REPS, 1)
    col = lane & (REPS - 1)
    other = jnp.where(row == col, 0.0, twice(upper[:, :REPS].T))
    half = last + pltpu.roll(last, REPS, 1)
    return upper + other + jnp.where(row == (col + 32) & (REPS - 1), half, 0.0)


def gram_kernel(place_ref, x_ref, small_ref, out_ref, wide):
    wide[...] = x_ref[...].astype(F32).reshape(REPS * TILE, HD)
    total = jnp.zeros((REPS, REPS), F32)
    for f in range(0, TILE, 2):
        rows = jnp.concatenate(
            [wide[pl.ds(f + e, REPS, stride=TILE), :].astype(BF16) for e in range(2)], axis=1
        )
        total = total + lax.dot_general(rows, rows, NT, preferred_element_type=F32)
    packed, last = pack_gram(total)
    own = [place_ref[0] == y for y in range(N_Y)]
    high, low = split(small_ref[...])
    rate = high[1:2] + pltpu.roll(low[1:2], REPS, 1)
    rates = jnp.where(own[0], rate, 0.0)
    for y in range(1, N_Y):
        rates = jnp.where(own[y], pltpu.roll(rate, 16 * y, 1), rates)
    gains = [jnp.where(own[y], part[0:1], 0.0) for part in (high, low) for y in range(N_Y)]
    block = jnp.concatenate([packed, last, rates, *gains, jnp.zeros((6, HD), F32)], axis=0)
    out_ref[...] = jnp.broadcast_to(block.astype(BF16)[None], out_ref.shape)


def split(value):
    high = value.astype(BF16).astype(F32)
    return high, value - high


def spread_kernel(in_ref, out_ref):
    total = in_ref[0].astype(F32)
    for m in range(1, N_Y * N_MP):
        total = total + in_ref[m].astype(F32)
    lane = lax.broadcasted_iota(jnp.int32, (1, HD), 1)
    rates = total[17:18] + pltpu.roll(total[17:18], REPS, 1)
    high, low = split(jnp.concatenate([rates, total[18:22] + total[22:26]], axis=0))
    rates = jnp.where(lane < REPS, high[0:1], low[0:1])
    block = jnp.concatenate(
        [total[0:17], rates, high[1:5], low[1:5], jnp.zeros((6, HD), F32)], axis=0
    )
    out_ref[...] = jnp.broadcast_to(block.astype(BF16)[None], out_ref.shape)


def small_tree(stack):
    half = REPS // 2
    while half:
        other = pltpu.roll(stack, half, 0)
        inner = jnp.sum(stack * other, axis=1, keepdims=True)
        norm = jnp.sum(stack * stack, axis=1, keepdims=True)
        part = (1.0 - inner / (2.0 * (norm + EPS))) * stack
        stack = part + pltpu.roll(part, half, 0)
        half //= 2
    return stack[0:1]


def trees_kernel(in_ref, gain_ref, rate_ref):
    lane = lax.broadcasted_iota(jnp.int32, (1, HD), 1)
    gains, rates = [], []
    for z in range(N_Z):
        block = in_ref[z].astype(F32)
        gains.append(block[18:22] + block[22:26])
        row = block[17:18]
        row = row + pltpu.roll(row, REPS, 1)
        for y in range(N_Y):
            rates.append(jnp.where(lane < 16, pltpu.roll(row, (-16 * y) % HD, 1), 0.0))
    gain_ref[...] = small_tree(jnp.concatenate(gains, axis=0))
    rate_ref[...] = small_tree(jnp.concatenate(rates, axis=0))


def path_coefs(gram):
    row, lane = places((REPS, HD))
    col = lane & (REPS - 1)
    first = lane < REPS

    def ratio(inner, norm):
        return 1.0 - inner / (2.0 * (norm + EPS))

    def pick(mask, axis):
        return jnp.sum(jnp.where(mask, gram, 0.0), axis=axis, keepdims=True)

    coefs = jnp.ones((REPS, 1), F32)
    half = REPS // 2
    same = row == col
    while half:
        across = row == (col + half) & (REPS - 1)
        by_col = ratio(pick(across & first, 1), pick(same & first, 1))
        by_row = ratio(pick(across, 0), pick(same, 0))
        coefs = coefs * by_col
        part = by_col * by_row * gram
        part = part + pltpu.roll(part, half, 1)
        gram = part + pltpu.roll(part, half, 0)
        half //= 2
    return coefs


def combine_kernel(in_ref, x_ref, out_ref, factor):
    total = in_ref[0].astype(F32)
    for z in range(1, N_Z):
        total = total + in_ref[z].astype(F32)
    gram = unpack_gram(total[0:16], total[16:17])
    factor[...] = jnp.broadcast_to(path_coefs(gram), (REPS, HD))
    total = jnp.zeros((TILE, HD), F32)
    for r in range(REPS):
        total = total + factor[r : r + 1, :] * x_ref[r].astype(F32)
    out_ref[...] = jnp.broadcast_to(total.astype(BF16)[None], out_ref.shape)


def unfold_kernel(in_ref, out_ref):
    for z in range(N_Z):
        out_ref[:, :, z * HD : (z + 1) * HD] = jnp.broadcast_to(
            in_ref[z][None], (N_Y, TILE, HD)
        )


def call(body, outs, ops, scratch=(), smem=(), hbm=(), out_hbm=(), flops=0, limit=LIMIT):
    size = sum(o.size * o.dtype.itemsize for o in ops) + sum(o.size * o.dtype.itemsize for o in outs)
    spaces = [
        pltpu.SMEM if i in smem else pl.ANY if i in hbm else pltpu.VMEM for i in range(len(ops))
    ]
    return pl.pallas_call(
        body,
        out_shape=outs,
        in_specs=[pl.BlockSpec(memory_space=space) for space in spaces],
        out_specs=[
            pl.BlockSpec(memory_space=pl.ANY if i in out_hbm else pltpu.VMEM)
            for i in range(len(outs))
        ],
        scratch_shapes=list(scratch),
        compiler_params=pltpu.CompilerParams(vmem_limit_bytes=limit),
        cost_estimate=pl.CostEstimate(flops=flops, bytes_accessed=size, transcendentals=0),
    )(*ops)


def shape(dims, dtype=F32):
    return jax.ShapeDtypeStruct(dims, dtype)


def forward(big, rows, gain_row):
    (tiles,) = call(
        forward_kernel,
        [shape((REPS, TILE, HD), BF16)],
        [*big, *rows, gain_row],
        scratch=[pltpu.VMEM(a.shape, BF16) for a in big]
        + [
            pltpu.VMEM((REPS, TILE, HD), BF16),
            pltpu.SemaphoreType.DMA((4,)),
            pltpu.SemaphoreType.DMA((N_Z,)),
        ],
        hbm=(0, 1, 2, 3),
        out_hbm=(0,),
        limit=56 * 2**20,
        flops=2 * 10**9,
    )
    return tiles


def backward(place, big, tiles, rows, gain_row):
    (small,) = call(
        backward_kernel,
        [shape((2, HD))],
        [place, *big, tiles, *rows, gain_row],
        scratch=[pltpu.VMEM(a.shape, BF16) for a in big] + [pltpu.SemaphoreType.DMA((5,))],
        smem=(0,),
        hbm=(1, 2, 3, 4, 5, 6),
        limit=56 * 2**20,
        flops=2 * 10**9,
    )
    return small


def gram(stack, small, place):
    (part,) = call(
        gram_kernel,
        [shape((N_Y * N_MP, 32, HD), BF16)],
        [place, stack, small],
        scratch=[pltpu.VMEM((REPS * TILE, HD), F32)],
        smem=(0,),
        flops=10**9,
    )
    return part


def combine(packed, stack):
    (tile,) = call(
        combine_kernel,
        [shape((N_Z, TILE, HD), BF16)],
        [packed, stack],
        scratch=[pltpu.VMEM((REPS, HD), F32)],
        flops=10**8,
    )
    return tile


def per_device(
    query_raw, key_raw, values, decay_input, beta_input, log_rate, step_bias, gain, out_weight, upstream
):
    gain_row = gain[None, :]
    big = (key_raw, query_raw, values, upstream)
    rows = (decay_input.T, beta_input.T, log_rate[None, :], step_bias[None, :])
    tiles = forward(big, rows, gain_row)
    stack = lax.all_to_all(tiles, "dp", 0, 0)
    place = lax.axis_index("mp").astype(jnp.int32)[None]
    small = backward(place, (*big, out_weight), tiles, rows, gain_row)
    place = (lax.axis_index("dp") % N_Y).astype(jnp.int32)[None]
    part = gram(stack, small, place)
    part = lax.all_to_all(part, ("dp", "mp"), 0, 0, axis_index_groups=PLANES)
    (part,) = call(spread_kernel, [shape((N_Z, 32, HD), BF16)], [part])
    packed = lax.all_to_all(part, "dp", 0, 0, axis_index_groups=Z_GROUPS)
    whole = combine(packed, stack)
    whole = lax.all_to_all(whole, "dp", 0, 0, axis_index_groups=Z_GROUPS)
    (whole,) = call(unfold_kernel, [shape((N_Y, TILE, N_Z * HD), BF16)], [whole])
    whole = lax.all_to_all(whole, "dp", 0, 0, axis_index_groups=Y_GROUPS)
    gain_final, rate_final = call(
        trees_kernel, [shape((1, HD)), shape((1, HD))], [packed]
    )
    return (
        whole.reshape(N_Y * TILE, N_Z * HD),
        gain_final[0],
        rate_final[0, : HEADS * N_MP],
    )


def solution(mesh):
    in_specs = (
        P("dp", "mp"),
        P("dp", "mp"),
        P("dp", "mp"),
        P("dp", "mp"),
        P("dp", "mp"),
        P("mp"),
        P("mp"),
        P(),
        P("mp", None),
        P("dp", None),
    )
    out_specs = (P("mp", None), P(), P())
    return jax.shard_map(
        per_device, mesh=mesh, in_specs=in_specs, out_specs=out_specs, check_vma=False
    )
```

```python
import functools

import jax
import jax.numpy as jnp
from jax import lax
from jax.experimental import pallas as pl
from jax.experimental.pallas import tpu as pltpu
from jax.sharding import PartitionSpec as P

EPS = 1e-06
F32 = jnp.float32
BF16 = jnp.bfloat16
HIGH = lax.Precision.HIGHEST
TOK = 128
HD = 128
HEADS = 2
REPS = 64
N_Z = 16
N_Y = 4
N_MP = 8
PAIR = 2 * N_Y
N_PAIRS = N_Z // 2
ROWS = 32
COLS = 256
LIMIT = 48 * 1024 * 1024
NN = (((1,), (0,)), ((), ()))
NT = (((1,), (1,)), ((), ()))

Z_GROUPS = [[z * N_Y + y for z in range(N_Z)] for y in range(N_Y)]
EVERY_OTHER = [
    [(z + i) * N_Y + y for z in range(0, N_Z, 2)] for i in range(2) for y in range(N_Y)
]
PAIRS = [[k * PAIR + i for i in range(PAIR)] for k in range(N_PAIRS)]
PLANES = [[z * N_Y * N_MP + i for i in range(N_Y * N_MP)] for z in range(N_Z)]


def matmul(a, b, dims=NN):
    return lax.dot_general(a, b, dims, precision=HIGH, preferred_element_type=F32)


def matmul3(a, b, dims=NN):
    ah, bh = a.astype(BF16), b.astype(BF16)
    al, bl = (a - ah.astype(F32)).astype(BF16), (b - bh.astype(F32)).astype(BF16)
    dot = functools.partial(lax.dot_general, dimension_numbers=dims, preferred_element_type=F32)
    return dot(ah, bh) + (dot(ah, bl) + dot(al, bh))


def places(shape):
    return (
        lax.broadcasted_iota(jnp.int32, shape, 0),
        lax.broadcasted_iota(jnp.int32, shape, 1),
    )


def unit_rows(raw):
    value = raw.astype(F32)
    return value / jnp.sqrt(jnp.sum(value * value, axis=-1, keepdims=True) + EPS)


def within(shift):
    row, col = places((TOK, TOK))
    return (row >> shift) == (col >> shift)


def invert_blocks(systems, mul):
    eye = within(0).astype(F32)
    first = [jnp.where(within(3), low, 0.0) for low in systems]
    second = [mul(a, a) for a in first]
    out = [eye - a for a in first]
    fourth = [mul(a, a) for a in second]
    out = [a + mul(a, b) for a, b in zip(out, second)]
    return [a + mul(a, b) for a, b in zip(out, fourth)]


def widen(systems, inverses, given, shift, mul):
    rest = within(shift + 2) & ~within(shift)
    steps = [mul(a, jnp.where(rest, low, 0.0)) for low, a in zip(systems, inverses)]
    out = inverses if given is None else [mul(a, v) for a, v in zip(inverses, given)]
    squares = [mul(a, a) for a in steps]
    out = [v - mul(a, v) for a, v in zip(steps, out)]
    return [v + mul(a, v) for a, v in zip(squares, out)]


def solve_all(systems, given, mul=matmul):
    inverses = widen(systems, invert_blocks(systems, mul), None, 3, mul)
    return widen(systems, inverses, given, 5, mul)


def small_inputs(dec_ref, beta_ref, rate_ref, bias_ref):
    row, col = places((TOK, TOK))
    falls = []
    for h in range(HEADS):
        pre = dec_ref[h : h + 1, :] + bias_ref[:, h : h + 1]
        soft = jnp.maximum(pre, 0.0) + jnp.log1p(jnp.exp(-jnp.abs(pre)))
        falls.append(-jnp.exp(rate_ref[:, h : h + 1]) * soft)
    cumul = matmul(jnp.concatenate(falls, axis=0), (row <= col).astype(F32))
    return cumul, 1.0 / (1.0 + jnp.exp(-beta_ref[...]))


def delta_parts(cumul, beta, inner, scores):
    row, col = places((TOK, TOK))
    lower = row >= col
    strict = row > col
    mixers, systems, spreads, strengths = [], [], [], []
    for h in range(HEADS):
        wide = jnp.broadcast_to(cumul[h : h + 1, :], (TOK, TOK))
        spread = jnp.where(lower, wide.T - wide, 0.0)
        decay = jnp.where(lower, jnp.exp(spread), 0.0)
        strength = jnp.broadcast_to(beta[h : h + 1, :], (TOK, TOK)).T
        mixers.append(scores * decay)
        systems.append(jnp.where(strict, strength * inner * decay, 0.0))
        spreads.append(spread)
        strengths.append(strength)
    return mixers, systems, spreads, strengths


def forward_kernel(
    k_any, q_any, v_any, up_any, dec_ref, beta_ref, rate_ref, bias_ref, gain_ref,
    g_any, k_ref, q_ref, v_ref, up_ref, g_ref, in_sems, out_sems,
):
    pairs = ((k_any, k_ref), (q_any, q_ref), (v_any, v_ref), (up_any, up_ref))
    fetches = [pltpu.make_async_copy(a, b, in_sems.at[i]) for i, (a, b) in enumerate(pairs)]
    for fetch in fetches:
        fetch.start()
    cumul, beta = small_inputs(dec_ref, beta_ref, rate_ref, bias_ref)
    heads = range(HEADS)
    fetches[0].wait()
    keys = unit_rows(k_ref[...])
    inner = matmul3(keys, keys, NT)
    fetches[1].wait()
    scores = matmul3(unit_rows(q_ref[...]) * HD ** (-0.5), keys, NT)
    mixers, systems, _, strengths = delta_parts(cumul, beta, inner, scores)
    fetches[2].wait()
    scaled = [strengths[h] * v_ref[:, h * HD : (h + 1) * HD].astype(F32) for h in heads]
    writes = solve_all(systems, scaled, matmul3)
    mixed = [matmul3(mixers[h], writes[h]) for h in heads]
    normed = []
    for h in heads:
        scale = lax.rsqrt(jnp.mean(mixed[h] * mixed[h], axis=-1, keepdims=True) + EPS)
        normed.append((mixed[h] * scale * gain_ref[...]).T.astype(BF16))
    left = jnp.concatenate(normed, axis=0)
    fetches[3].wait()
    stores = []
    for k in range(N_PAIRS):
        part = lax.dot_general(
            left, up_ref[:, k * COLS : (k + 1) * COLS], NN, preferred_element_type=F32
        ).astype(BF16)
        for i in range(PAIR):
            g_ref[k * PAIR + i] = part[i * ROWS : (i + 1) * ROWS, :]
        tiles = pl.ds(k * PAIR, PAIR)
        stores.append(pltpu.make_async_copy(g_ref.at[tiles], g_any.at[tiles], out_sems.at[k]))
        stores[k].start()
    for store in stores:
        store.wait()


def backward_kernel(
    place_ref, k_any, q_any, v_any, up_any, weight_any, _, dec_ref, beta_ref, rate_ref, bias_ref,
    gain_ref, out_ref, k_ref, q_ref, v_ref, up_ref, weight_ref, in_sems,
):
    pairs = (
        (k_any, k_ref), (q_any, q_ref), (v_any, v_ref), (up_any, up_ref), (weight_any, weight_ref)
    )
    fetches = [pltpu.make_async_copy(a, b, in_sems.at[i]) for i, (a, b) in enumerate(pairs)]
    for fetch in fetches:
        fetch.start()
    for fetch in fetches:
        fetch.wait()
    gain = gain_ref[...]
    d_normed = lax.dot_general(up_ref[...], weight_ref[...], NT, preferred_element_type=F32)
    lane = lax.broadcasted_iota(jnp.int32, (1, HD), 1)
    heads = range(HEADS)
    keys = unit_rows(k_ref[...])
    inner = matmul(keys, keys, NT)
    scores = matmul(unit_rows(q_ref[...]) * HD ** (-0.5), keys, NT)
    cumul, beta = small_inputs(dec_ref, beta_ref, rate_ref, bias_ref)
    mixers, systems, spreads, strengths = delta_parts(cumul, beta, inner, scores)
    scaled = [strengths[h] * v_ref[:, h * HD : (h + 1) * HD].astype(F32) for h in heads]
    writes = solve_all(systems, scaled)
    outs = [matmul(mixers[h], writes[h]) for h in heads]
    turns = solve_all(systems, [matmul(systems[h] * spreads[h], writes[h]) for h in heads])
    slopes = [
        matmul(mixers[h] * spreads[h], writes[h]) - matmul(mixers[h], turns[h]) for h in heads
    ]
    grad_gain = jnp.zeros((1, HD), F32)
    rates = jnp.zeros((1, HD), F32)
    for h in heads:
        mixed = outs[h]
        scale = lax.rsqrt(jnp.mean(mixed * mixed, axis=-1, keepdims=True) + EPS)
        unit = mixed * scale
        given = d_normed[:, h * HD : (h + 1) * HD]
        grad_gain = grad_gain + jnp.sum(unit * given, axis=0, keepdims=True)
        tilted = given * gain
        d_mixed = scale * (tilted - unit * jnp.mean(unit * tilted, axis=-1, keepdims=True))
        rate = jnp.sum(jnp.sum(d_mixed * slopes[h], axis=0, keepdims=True), axis=1, keepdims=True)
        rates = rates + jnp.where(lane == place_ref[0] * HEADS + h, rate, 0.0)
    out_ref[...] = jnp.concatenate([grad_gain, rates], axis=0)


def turn_left(value):
    row, _ = places(value.shape)
    parts = []
    for g in range(REPS // 8):
        part = value[8 * g : 8 * g + 8]
        parts.append(pltpu.roll(part, HD - 8 * g, 1) if g else part)
    value = jnp.concatenate(parts, axis=0)
    for bit in range(3):
        value = jnp.where((row >> bit) & 1 == 1, pltpu.roll(value, HD - 2**bit, 1), value)
    return value


def turn_right(value):
    parts = [
        pltpu.roll(value[8 * g : 8 * g + 8], 8 * g, 1, stride=1, stride_axis=0)
        for g in range(REPS // 8)
    ]
    return jnp.concatenate(parts, axis=0)


def twice(value):
    return jnp.concatenate([value, value], axis=1)


def pack_gram(total):
    row, lane = places((REPS, HD))
    wide = twice(total)
    turned = turn_left(wide)
    _, slot = places((16, HD))
    packed = turned[0:16]
    for q in range(1, 4):
        packed = jnp.where(
            slot >> 5 == q, pltpu.roll(turned[16 * q : 16 * q + 16], 32 * q, 1), packed
        )
    across = (lane < REPS) & (row == (lane + 32) & (REPS - 1))
    return packed, jnp.sum(jnp.where(across, wide, 0.0), axis=0, keepdims=True)


def unpack_gram(packed, last):
    row, lane = places((REPS, HD))
    turned = jnp.concatenate(
        [packed] + [pltpu.roll(packed, HD - 32 * q, 1) for q in range(1, 4)], axis=0
    )
    upper = turn_right(jnp.where(lane < 32, turned, 0.0))
    upper = upper + pltpu.roll(upper, REPS, 1)
    col = lane & (REPS - 1)
    other = jnp.where(row == col, 0.0, twice(upper[:, :REPS].T))
    half = last + pltpu.roll(last, REPS, 1)
    return upper + other + jnp.where(row == (col + 32) & (REPS - 1), half, 0.0)


def gram_kernel(place_ref, x_ref, small_ref, out_ref, wide):
    for e in range(2):
        wide[e] = x_ref[:, :, e * HD : (e + 1) * HD].astype(F32).reshape(REPS * ROWS, HD)
    total = jnp.zeros((REPS, REPS), F32)
    for f in range(ROWS):
        rows = jnp.concatenate(
            [wide[e, pl.ds(f, REPS, stride=ROWS), :].astype(BF16) for e in range(2)], axis=1
        )
        total = total + lax.dot_general(rows, rows, NT, preferred_element_type=F32)
    packed, last = pack_gram(total)
    own = [place_ref[0] == y for y in range(N_Y)]
    high, low = split(small_ref[...])
    rate = high[1:2] + pltpu.roll(low[1:2], REPS, 1)
    rates = jnp.where(own[0], rate, 0.0)
    for y in range(1, N_Y):
        rates = jnp.where(own[y], pltpu.roll(rate, 16 * y, 1), rates)
    gains = [jnp.where(own[y], part[0:1], 0.0) for part in (high, low) for y in range(N_Y)]
    block = jnp.concatenate([packed, last, rates, *gains, jnp.zeros((6, HD), F32)], axis=0)
    out_ref[...] = jnp.broadcast_to(block.astype(BF16)[None], out_ref.shape)


def split(value):
    high = value.astype(BF16).astype(F32)
    return high, value - high


def spread_kernel(in_ref, out_ref):
    total = in_ref[0].astype(F32)
    for m in range(1, N_Y * N_MP):
        total = total + in_ref[m].astype(F32)
    lane = lax.broadcasted_iota(jnp.int32, (1, HD), 1)
    rates = total[17:18] + pltpu.roll(total[17:18], REPS, 1)
    high, low = split(jnp.concatenate([rates, total[18:22] + total[22:26]], axis=0))
    rates = jnp.where(lane < REPS, high[0:1], low[0:1])
    block = jnp.concatenate(
        [total[0:17], rates, high[1:5], low[1:5], jnp.zeros((6, HD), F32)], axis=0
    )
    out_ref[...] = jnp.broadcast_to(block.astype(BF16)[None], out_ref.shape)


def small_tree(stack):
    half = REPS // 2
    while half:
        other = pltpu.roll(stack, half, 0)
        inner = jnp.sum(stack * other, axis=1, keepdims=True)
        norm = jnp.sum(stack * stack, axis=1, keepdims=True)
        part = (1.0 - inner / (2.0 * (norm + EPS))) * stack
        stack = part + pltpu.roll(part, half, 0)
        half //= 2
    return stack[0:1]


def trees_kernel(in_ref, gain_ref, rate_ref):
    lane = lax.broadcasted_iota(jnp.int32, (1, HD), 1)
    gains, rates = [], []
    for z in range(N_Z):
        block = in_ref[z].astype(F32)
        gains.append(block[18:22] + block[22:26])
        row = block[17:18]
        row = row + pltpu.roll(row, REPS, 1)
        for y in range(N_Y):
            rates.append(jnp.where(lane < 16, pltpu.roll(row, (-16 * y) % HD, 1), 0.0))
    gain_ref[...] = small_tree(jnp.concatenate(gains, axis=0))
    rate_ref[...] = small_tree(jnp.concatenate(rates, axis=0))


def path_coefs(gram):
    row, lane = places((REPS, HD))
    col = lane & (REPS - 1)
    first = lane < REPS

    def ratio(inner, norm):
        return 1.0 - inner / (2.0 * (norm + EPS))

    def pick(mask, axis):
        return jnp.sum(jnp.where(mask, gram, 0.0), axis=axis, keepdims=True)

    coefs = jnp.ones((REPS, 1), F32)
    half = REPS // 2
    same = row == col
    while half:
        across = row == (col + half) & (REPS - 1)
        by_col = ratio(pick(across & first, 1), pick(same & first, 1))
        by_row = ratio(pick(across, 0), pick(same, 0))
        coefs = coefs * by_col
        part = by_col * by_row * gram
        part = part + pltpu.roll(part, half, 1)
        gram = part + pltpu.roll(part, half, 0)
        half //= 2
    return coefs


def combine_kernel(in_ref, x_ref, out_ref, factor):
    total = in_ref[0].astype(F32)
    for z in range(1, N_Z):
        total = total + in_ref[z].astype(F32)
    gram = unpack_gram(total[0:16], total[16:17])
    factor[...] = jnp.broadcast_to(path_coefs(gram), (REPS, COLS))
    total = jnp.zeros((ROWS, COLS), F32)
    for r in range(REPS):
        total = total + factor[r : r + 1, :] * x_ref[r].astype(F32)
    out_ref[...] = jnp.broadcast_to(total.astype(BF16)[None], out_ref.shape)


def unfold_kernel(in_ref, out_ref):
    for k in range(N_PAIRS):
        out_ref[:, :, k * COLS : (k + 1) * COLS] = jnp.broadcast_to(
            in_ref[k][None], (PAIR, ROWS, COLS)
        )


def call(body, outs, ops, scratch=(), smem=(), hbm=(), out_hbm=(), flops=0, limit=LIMIT):
    size = sum(o.size * o.dtype.itemsize for o in ops) + sum(o.size * o.dtype.itemsize for o in outs)
    spaces = [
        pltpu.SMEM if i in smem else pl.ANY if i in hbm else pltpu.VMEM for i in range(len(ops))
    ]
    return pl.pallas_call(
        body,
        out_shape=outs,
        in_specs=[pl.BlockSpec(memory_space=space) for space in spaces],
        out_specs=[
            pl.BlockSpec(memory_space=pl.ANY if i in out_hbm else pltpu.VMEM)
            for i in range(len(outs))
        ],
        scratch_shapes=list(scratch),
        compiler_params=pltpu.CompilerParams(vmem_limit_bytes=limit),
        cost_estimate=pl.CostEstimate(flops=flops, bytes_accessed=size, transcendentals=0),
    )(*ops)


def shape(dims, dtype=F32):
    return jax.ShapeDtypeStruct(dims, dtype)


def forward(big, rows, gain_row):
    (tiles,) = call(
        forward_kernel,
        [shape((REPS, ROWS, COLS), BF16)],
        [*big, *rows, gain_row],
        scratch=[pltpu.VMEM(a.shape, BF16) for a in big]
        + [
            pltpu.VMEM((REPS, ROWS, COLS), BF16),
            pltpu.SemaphoreType.DMA((4,)),
            pltpu.SemaphoreType.DMA((N_PAIRS,)),
        ],
        hbm=(0, 1, 2, 3),
        out_hbm=(0,),
        limit=56 * 2**20,
        flops=2 * 10**9,
    )
    return tiles


def backward(place, big, tiles, rows, gain_row):
    (small,) = call(
        backward_kernel,
        [shape((2, HD))],
        [place, *big, tiles, *rows, gain_row],
        scratch=[pltpu.VMEM(a.shape, BF16) for a in big] + [pltpu.SemaphoreType.DMA((5,))],
        smem=(0,),
        hbm=(1, 2, 3, 4, 5, 6),
        limit=56 * 2**20,
        flops=2 * 10**9,
    )
    return small


def gram(stack, small, place):
    (part,) = call(
        gram_kernel,
        [shape((N_Y * N_MP, 32, HD), BF16)],
        [place, stack, small],
        scratch=[pltpu.VMEM((2, REPS * ROWS, HD), F32)],
        smem=(0,),
        flops=10**9,
    )
    return part


def combine(packed, stack):
    (tile,) = call(
        combine_kernel,
        [shape((N_PAIRS, ROWS, COLS), BF16)],
        [packed, stack],
        scratch=[pltpu.VMEM((REPS, COLS), F32)],
        flops=10**8,
    )
    return tile


def per_device(
    query_raw, key_raw, values, decay_input, beta_input, log_rate, step_bias, gain, out_weight, upstream
):
    gain_row = gain[None, :]
    big = (key_raw, query_raw, values, upstream)
    rows = (decay_input.T, beta_input.T, log_rate[None, :], step_bias[None, :])
    tiles = forward(big, rows, gain_row)
    stack = lax.all_to_all(tiles, "dp", 0, 0)
    place = lax.axis_index("mp").astype(jnp.int32)[None]
    small = backward(place, (*big, out_weight), tiles, rows, gain_row)
    place = (lax.axis_index("dp") % N_Y).astype(jnp.int32)[None]
    part = gram(stack, small, place)
    part = lax.all_to_all(part, ("dp", "mp"), 0, 0, axis_index_groups=PLANES)
    (part,) = call(spread_kernel, [shape((N_Z, 32, HD), BF16)], [part])
    packed = lax.all_to_all(part, "dp", 0, 0, axis_index_groups=Z_GROUPS)
    whole = combine(packed, stack)
    whole = lax.all_to_all(whole, "dp", 0, 0, axis_index_groups=EVERY_OTHER)
    (whole,) = call(unfold_kernel, [shape((PAIR, ROWS, N_PAIRS * COLS), BF16)], [whole])
    whole = lax.all_to_all(whole, "dp", 0, 0, axis_index_groups=PAIRS)
    gain_final, rate_final = call(
        trees_kernel, [shape((1, HD)), shape((1, HD))], [packed]
    )
    return (
        whole.reshape(PAIR * ROWS, N_PAIRS * COLS),
        gain_final[0],
        rate_final[0, : HEADS * N_MP],
    )


def solution(mesh):
    in_specs = (
        P("dp", "mp"),
        P("dp", "mp"),
        P("dp", "mp"),
        P("dp", "mp"),
        P("dp", "mp"),
        P("mp"),
        P("mp"),
        P(),
        P("mp", None),
        P("dp", None),
    )
    out_specs = (P("mp", None), P(), P())
    return jax.shard_map(
        per_device, mesh=mesh, in_specs=in_specs, out_specs=out_specs, check_vma=False
    )
```

```python
import functools

import jax
import jax.numpy as jnp
from jax import lax
from jax.experimental import pallas as pl
from jax.experimental.pallas import tpu as pltpu
from jax.sharding import PartitionSpec as P

EPS = 1e-06
F32 = jnp.float32
BF16 = jnp.bfloat16
HIGH = lax.Precision.HIGHEST
TOK = 128
HD = 128
HEADS = 2
REPS = 64
N_Z = 16
N_Y = 4
N_MP = 8
PAIR = 2 * N_Y
N_PAIRS = N_Z // 2
ROWS = 32
COLS = 256
PITCH = 36
LIMIT = 48 * 1024 * 1024
NN = (((1,), (0,)), ((), ()))
NT = (((1,), (1,)), ((), ()))

Z_GROUPS = [[z * N_Y + y for z in range(N_Z)] for y in range(N_Y)]
EVERY_OTHER = [
    [(z + i) * N_Y + y for z in range(0, N_Z, 2)] for i in range(2) for y in range(N_Y)
]
PAIRS = [[k * PAIR + i for i in range(PAIR)] for k in range(N_PAIRS)]
PLANES = [[z * N_Y * N_MP + i for i in range(N_Y * N_MP)] for z in range(N_Z)]


def matmul(a, b, dims=NN):
    return lax.dot_general(a, b, dims, precision=HIGH, preferred_element_type=F32)


def matmul3(a, b, dims=NN):
    ah, bh = a.astype(BF16), b.astype(BF16)
    al, bl = (a - ah.astype(F32)).astype(BF16), (b - bh.astype(F32)).astype(BF16)
    dot = functools.partial(lax.dot_general, dimension_numbers=dims, preferred_element_type=F32)
    return dot(ah, bh) + (dot(ah, bl) + dot(al, bh))


def places(shape):
    return (
        lax.broadcasted_iota(jnp.int32, shape, 0),
        lax.broadcasted_iota(jnp.int32, shape, 1),
    )


def unit_rows(raw):
    value = raw.astype(F32)
    return value / jnp.sqrt(jnp.sum(value * value, axis=-1, keepdims=True) + EPS)


def within(shift):
    row, col = places((TOK, TOK))
    return (row >> shift) == (col >> shift)


def invert_blocks(systems, mul):
    eye = within(0).astype(F32)
    first = [jnp.where(within(3), low, 0.0) for low in systems]
    second = [mul(a, a) for a in first]
    out = [eye - a for a in first]
    fourth = [mul(a, a) for a in second]
    out = [a + mul(a, b) for a, b in zip(out, second)]
    return [a + mul(a, b) for a, b in zip(out, fourth)]


def widen(systems, inverses, given, shift, mul):
    rest = within(shift + 2) & ~within(shift)
    steps = [mul(a, jnp.where(rest, low, 0.0)) for low, a in zip(systems, inverses)]
    out = inverses if given is None else [mul(a, v) for a, v in zip(inverses, given)]
    squares = [mul(a, a) for a in steps]
    out = [v - mul(a, v) for a, v in zip(steps, out)]
    return [v + mul(a, v) for a, v in zip(squares, out)]


def solve_all(systems, given, mul=matmul):
    inverses = widen(systems, invert_blocks(systems, mul), None, 3, mul)
    return widen(systems, inverses, given, 5, mul)


def small_inputs(dec_ref, beta_ref, rate_ref, bias_ref):
    row, col = places((TOK, TOK))
    falls = []
    for h in range(HEADS):
        pre = dec_ref[h : h + 1, :] + bias_ref[:, h : h + 1]
        soft = jnp.maximum(pre, 0.0) + jnp.log1p(jnp.exp(-jnp.abs(pre)))
        falls.append(-jnp.exp(rate_ref[:, h : h + 1]) * soft)
    cumul = matmul(jnp.concatenate(falls, axis=0), (row <= col).astype(F32))
    return cumul, 1.0 / (1.0 + jnp.exp(-beta_ref[...]))


def delta_parts(cumul, beta, inner, scores):
    row, col = places((TOK, TOK))
    lower = row >= col
    strict = row > col
    mixers, systems, spreads, strengths = [], [], [], []
    for h in range(HEADS):
        wide = jnp.broadcast_to(cumul[h : h + 1, :], (TOK, TOK))
        spread = jnp.where(lower, wide.T - wide, 0.0)
        decay = jnp.where(lower, jnp.exp(spread), 0.0)
        strength = jnp.broadcast_to(beta[h : h + 1, :], (TOK, TOK)).T
        mixers.append(scores * decay)
        systems.append(jnp.where(strict, strength * inner * decay, 0.0))
        spreads.append(spread)
        strengths.append(strength)
    return mixers, systems, spreads, strengths


def forward_kernel(
    k_any, q_any, v_any, up_any, dec_ref, beta_ref, rate_ref, bias_ref, gain_ref,
    g_any, k_ref, q_ref, v_ref, up_ref, g_ref, in_sems, out_sems,
):
    pairs = ((k_any, k_ref), (q_any, q_ref), (v_any, v_ref), (up_any, up_ref))
    fetches = [pltpu.make_async_copy(a, b, in_sems.at[i]) for i, (a, b) in enumerate(pairs)]
    for fetch in fetches:
        fetch.start()
    cumul, beta = small_inputs(dec_ref, beta_ref, rate_ref, bias_ref)
    heads = range(HEADS)
    fetches[0].wait()
    keys = unit_rows(k_ref[...])
    inner = matmul3(keys, keys, NT)
    fetches[1].wait()
    scores = matmul3(unit_rows(q_ref[...]) * HD ** (-0.5), keys, NT)
    mixers, systems, _, strengths = delta_parts(cumul, beta, inner, scores)
    fetches[2].wait()
    scaled = [strengths[h] * v_ref[:, h * HD : (h + 1) * HD].astype(F32) for h in heads]
    writes = solve_all(systems, scaled, matmul3)
    mixed = [matmul3(mixers[h], writes[h]) for h in heads]
    normed = []
    for h in heads:
        scale = lax.rsqrt(jnp.mean(mixed[h] * mixed[h], axis=-1, keepdims=True) + EPS)
        normed.append((mixed[h] * scale * gain_ref[...]).T.astype(BF16))
    left = jnp.concatenate(normed, axis=0)
    fetches[3].wait()
    stores = []
    for k in range(N_PAIRS):
        part = lax.dot_general(
            left, up_ref[:, k * COLS : (k + 1) * COLS], NN, preferred_element_type=F32
        ).astype(BF16)
        for i in range(PAIR):
            g_ref[k * PAIR + i] = part[i * ROWS : (i + 1) * ROWS, :]
        tiles = pl.ds(k * PAIR, PAIR)
        stores.append(pltpu.make_async_copy(g_ref.at[tiles], g_any.at[tiles], out_sems.at[k]))
        stores[k].start()
    for store in stores:
        store.wait()


def backward_kernel(
    place_ref, k_any, q_any, v_any, up_any, weight_any, _, dec_ref, beta_ref, rate_ref, bias_ref,
    gain_ref, out_ref, k_ref, q_ref, v_ref, up_ref, weight_ref, in_sems,
):
    pairs = (
        (k_any, k_ref), (q_any, q_ref), (v_any, v_ref), (up_any, up_ref), (weight_any, weight_ref)
    )
    fetches = [pltpu.make_async_copy(a, b, in_sems.at[i]) for i, (a, b) in enumerate(pairs)]
    for fetch in fetches:
        fetch.start()
    for fetch in fetches:
        fetch.wait()
    gain = gain_ref[...]
    d_normed = lax.dot_general(up_ref[...], weight_ref[...], NT, preferred_element_type=F32)
    lane = lax.broadcasted_iota(jnp.int32, (1, HD), 1)
    heads = range(HEADS)
    keys = unit_rows(k_ref[...])
    inner = matmul(keys, keys, NT)
    scores = matmul(unit_rows(q_ref[...]) * HD ** (-0.5), keys, NT)
    cumul, beta = small_inputs(dec_ref, beta_ref, rate_ref, bias_ref)
    mixers, systems, spreads, strengths = delta_parts(cumul, beta, inner, scores)
    scaled = [strengths[h] * v_ref[:, h * HD : (h + 1) * HD].astype(F32) for h in heads]
    writes = solve_all(systems, scaled)
    outs = [matmul(mixers[h], writes[h]) for h in heads]
    turns = solve_all(systems, [matmul(systems[h] * spreads[h], writes[h]) for h in heads])
    slopes = [
        matmul(mixers[h] * spreads[h], writes[h]) - matmul(mixers[h], turns[h]) for h in heads
    ]
    grad_gain = jnp.zeros((1, HD), F32)
    rates = jnp.zeros((1, HD), F32)
    for h in heads:
        mixed = outs[h]
        scale = lax.rsqrt(jnp.mean(mixed * mixed, axis=-1, keepdims=True) + EPS)
        unit = mixed * scale
        given = d_normed[:, h * HD : (h + 1) * HD]
        grad_gain = grad_gain + jnp.sum(unit * given, axis=0, keepdims=True)
        tilted = given * gain
        d_mixed = scale * (tilted - unit * jnp.mean(unit * tilted, axis=-1, keepdims=True))
        rate = jnp.sum(jnp.sum(d_mixed * slopes[h], axis=0, keepdims=True), axis=1, keepdims=True)
        rates = rates + jnp.where(lane == place_ref[0] * HEADS + h, rate, 0.0)
    out_ref[...] = jnp.concatenate([grad_gain, rates], axis=0)


def turn_left(value):
    row, _ = places(value.shape)
    parts = []
    for g in range(REPS // 8):
        part = value[8 * g : 8 * g + 8]
        parts.append(pltpu.roll(part, HD - 8 * g, 1) if g else part)
    value = jnp.concatenate(parts, axis=0)
    for bit in range(3):
        value = jnp.where((row >> bit) & 1 == 1, pltpu.roll(value, HD - 2**bit, 1), value)
    return value


def turn_right(value):
    parts = [
        pltpu.roll(value[8 * g : 8 * g + 8], 8 * g, 1, stride=1, stride_axis=0)
        for g in range(REPS // 8)
    ]
    return jnp.concatenate(parts, axis=0)


def twice(value):
    return jnp.concatenate([value, value], axis=1)


def pack_gram(total):
    row, lane = places((REPS, HD))
    wide = twice(total)
    turned = turn_left(wide)
    _, slot = places((16, HD))
    packed = turned[0:16]
    for q in range(1, 4):
        packed = jnp.where(
            slot >> 5 == q, pltpu.roll(turned[16 * q : 16 * q + 16], 32 * q, 1), packed
        )
    across = (lane < REPS) & (row == (lane + 32) & (REPS - 1))
    return packed, jnp.sum(jnp.where(across, wide, 0.0), axis=0, keepdims=True)


def unpack_gram(packed, last):
    row, lane = places((REPS, HD))
    turned = jnp.concatenate(
        [packed] + [pltpu.roll(packed, HD - 32 * q, 1) for q in range(1, 4)], axis=0
    )
    upper = turn_right(jnp.where(lane < 32, turned, 0.0))
    upper = upper + pltpu.roll(upper, REPS, 1)
    col = lane & (REPS - 1)
    other = jnp.where(row == col, 0.0, twice(upper[:, :REPS].T))
    half = last + pltpu.roll(last, REPS, 1)
    return upper + other + jnp.where(row == (col + 32) & (REPS - 1), half, 0.0)


def gram_kernel(place_ref, x_ref, small_ref, out_ref, wide):
    for e in range(2):
        for r in range(REPS):
            wide[e, pl.ds(r * PITCH, ROWS), :] = x_ref[r, :, e * HD : (e + 1) * HD].astype(F32)
    total = jnp.zeros((REPS, REPS), F32)
    for f in range(ROWS):
        rows = jnp.concatenate(
            [wide[e, pl.ds(f, REPS, stride=PITCH), :].astype(BF16) for e in range(2)], axis=1
        )
        total = total + lax.dot_general(rows, rows, NT, preferred_element_type=F32)
    packed, last = pack_gram(total)
    own = [place_ref[0] == y for y in range(N_Y)]
    high, low = split(small_ref[...])
    rate = high[1:2] + pltpu.roll(low[1:2], REPS, 1)
    rates = jnp.where(own[0], rate, 0.0)
    for y in range(1, N_Y):
        rates = jnp.where(own[y], pltpu.roll(rate, 16 * y, 1), rates)
    gains = [jnp.where(own[y], part[0:1], 0.0) for part in (high, low) for y in range(N_Y)]
    block = jnp.concatenate([packed, last, rates, *gains, jnp.zeros((6, HD), F32)], axis=0)
    out_ref[...] = jnp.broadcast_to(block.astype(BF16)[None], out_ref.shape)


def split(value):
    high = value.astype(BF16).astype(F32)
    return high, value - high


def spread_kernel(in_ref, out_ref):
    total = in_ref[0].astype(F32)
    for m in range(1, N_Y * N_MP):
        total = total + in_ref[m].astype(F32)
    lane = lax.broadcasted_iota(jnp.int32, (1, HD), 1)
    rates = total[17:18] + pltpu.roll(total[17:18], REPS, 1)
    high, low = split(jnp.concatenate([rates, total[18:22] + total[22:26]], axis=0))
    rates = jnp.where(lane < REPS, high[0:1], low[0:1])
    block = jnp.concatenate(
        [total[0:17], rates, high[1:5], low[1:5], jnp.zeros((6, HD), F32)], axis=0
    )
    out_ref[...] = jnp.broadcast_to(block.astype(BF16)[None], out_ref.shape)


def small_tree(stack):
    half = REPS // 2
    while half:
        other = pltpu.roll(stack, half, 0)
        inner = jnp.sum(stack * other, axis=1, keepdims=True)
        norm = jnp.sum(stack * stack, axis=1, keepdims=True)
        part = (1.0 - inner / (2.0 * (norm + EPS))) * stack
        stack = part + pltpu.roll(part, half, 0)
        half //= 2
    return stack[0:1]


def trees_kernel(in_ref, gain_ref, rate_ref):
    lane = lax.broadcasted_iota(jnp.int32, (1, HD), 1)
    gains, rates = [], []
    for z in range(N_Z):
        block = in_ref[z].astype(F32)
        gains.append(block[18:22] + block[22:26])
        row = block[17:18]
        row = row + pltpu.roll(row, REPS, 1)
        for y in range(N_Y):
            rates.append(jnp.where(lane < 16, pltpu.roll(row, (-16 * y) % HD, 1), 0.0))
    gain_ref[...] = small_tree(jnp.concatenate(gains, axis=0))
    rate_ref[...] = small_tree(jnp.concatenate(rates, axis=0))


def path_coefs(gram):
    row, lane = places((REPS, HD))
    col = lane & (REPS - 1)
    first = lane < REPS

    def ratio(inner, norm):
        return 1.0 - inner / (2.0 * (norm + EPS))

    def pick(mask, axis):
        return jnp.sum(jnp.where(mask, gram, 0.0), axis=axis, keepdims=True)

    coefs = jnp.ones((REPS, 1), F32)
    half = REPS // 2
    same = row == col
    while half:
        across = row == (col + half) & (REPS - 1)
        by_col = ratio(pick(across & first, 1), pick(same & first, 1))
        by_row = ratio(pick(across, 0), pick(same, 0))
        coefs = coefs * by_col
        part = by_col * by_row * gram
        part = part + pltpu.roll(part, half, 1)
        gram = part + pltpu.roll(part, half, 0)
        half //= 2
    return coefs


def combine_kernel(in_ref, x_ref, out_ref, factor):
    total = in_ref[0].astype(F32)
    for z in range(1, N_Z):
        total = total + in_ref[z].astype(F32)
    gram = unpack_gram(total[0:16], total[16:17])
    factor[...] = jnp.broadcast_to(path_coefs(gram), (REPS, COLS))
    total = jnp.zeros((ROWS, COLS), F32)
    for r in range(REPS):
        total = total + factor[r : r + 1, :] * x_ref[r].astype(F32)
    out_ref[...] = jnp.broadcast_to(total.astype(BF16)[None], out_ref.shape)


def unfold_kernel(in_ref, out_any, line_ref, sems):
    for k in range(N_PAIRS):
        line_ref[:, k * COLS : (k + 1) * COLS] = in_ref[k]
    stores = [pltpu.make_async_copy(line_ref, out_any.at[i], sems.at[i]) for i in range(PAIR)]
    for store in stores:
        store.start()
    for store in stores:
        store.wait()


def unfold(tiles):
    (out,) = call(
        unfold_kernel,
        [shape((PAIR, ROWS, N_PAIRS * COLS), BF16)],
        [tiles],
        scratch=[pltpu.VMEM((ROWS, N_PAIRS * COLS), BF16), pltpu.SemaphoreType.DMA((PAIR,))],
        out_hbm=(0,),
    )
    return out


def call(body, outs, ops, scratch=(), smem=(), hbm=(), out_hbm=(), flops=0, limit=LIMIT):
    size = sum(o.size * o.dtype.itemsize for o in ops) + sum(o.size * o.dtype.itemsize for o in outs)
    spaces = [
        pltpu.SMEM if i in smem else pl.ANY if i in hbm else pltpu.VMEM for i in range(len(ops))
    ]
    return pl.pallas_call(
        body,
        out_shape=outs,
        in_specs=[pl.BlockSpec(memory_space=space) for space in spaces],
        out_specs=[
            pl.BlockSpec(memory_space=pl.ANY if i in out_hbm else pltpu.VMEM)
            for i in range(len(outs))
        ],
        scratch_shapes=list(scratch),
        compiler_params=pltpu.CompilerParams(vmem_limit_bytes=limit),
        cost_estimate=pl.CostEstimate(flops=flops, bytes_accessed=size, transcendentals=0),
    )(*ops)


def shape(dims, dtype=F32):
    return jax.ShapeDtypeStruct(dims, dtype)


def forward(big, rows, gain_row):
    (tiles,) = call(
        forward_kernel,
        [shape((REPS, ROWS, COLS), BF16)],
        [*big, *rows, gain_row],
        scratch=[pltpu.VMEM(a.shape, BF16) for a in big]
        + [
            pltpu.VMEM((REPS, ROWS, COLS), BF16),
            pltpu.SemaphoreType.DMA((4,)),
            pltpu.SemaphoreType.DMA((N_PAIRS,)),
        ],
        hbm=(0, 1, 2, 3),
        out_hbm=(0,),
        limit=56 * 2**20,
        flops=2 * 10**9,
    )
    return tiles


def backward(place, big, tiles, rows, gain_row):
    (small,) = call(
        backward_kernel,
        [shape((2, HD))],
        [place, *big, tiles, *rows, gain_row],
        scratch=[pltpu.VMEM(a.shape, BF16) for a in big] + [pltpu.SemaphoreType.DMA((5,))],
        smem=(0,),
        hbm=(1, 2, 3, 4, 5, 6),
        limit=56 * 2**20,
        flops=2 * 10**9,
    )
    return small


def gram(stack, small, place):
    (part,) = call(
        gram_kernel,
        [shape((N_Y * N_MP, 32, HD), BF16)],
        [place, stack, small],
        scratch=[pltpu.VMEM((2, REPS * PITCH + 64, HD), F32)],
        smem=(0,),
        flops=10**9,
    )
    return part


def combine(packed, stack):
    (tile,) = call(
        combine_kernel,
        [shape((N_PAIRS, ROWS, COLS), BF16)],
        [packed, stack],
        scratch=[pltpu.VMEM((REPS, COLS), F32)],
        flops=10**8,
    )
    return tile


def per_device(
    query_raw, key_raw, values, decay_input, beta_input, log_rate, step_bias, gain, out_weight, upstream
):
    gain_row = gain[None, :]
    big = (key_raw, query_raw, values, upstream)
    rows = (decay_input.T, beta_input.T, log_rate[None, :], step_bias[None, :])
    tiles = forward(big, rows, gain_row)
    stack = lax.all_to_all(tiles, "dp", 0, 0)
    place = lax.axis_index("mp").astype(jnp.int32)[None]
    small = backward(place, (*big, out_weight), tiles, rows, gain_row)
    place = (lax.axis_index("dp") % N_Y).astype(jnp.int32)[None]
    part = gram(stack, small, place)
    part = lax.all_to_all(part, ("dp", "mp"), 0, 0, axis_index_groups=PLANES)
    (part,) = call(spread_kernel, [shape((N_Z, 32, HD), BF16)], [part])
    packed = lax.all_to_all(part, "dp", 0, 0, axis_index_groups=Z_GROUPS)
    whole = combine(packed, stack)
    whole = lax.all_to_all(whole, "dp", 0, 0, axis_index_groups=EVERY_OTHER)
    whole = unfold(whole)
    whole = lax.all_to_all(whole, "dp", 0, 0, axis_index_groups=PAIRS)
    gain_final, rate_final = call(
        trees_kernel, [shape((1, HD)), shape((1, HD))], [packed]
    )
    return (
        whole.reshape(PAIR * ROWS, N_PAIRS * COLS),
        gain_final[0],
        rate_final[0, : HEADS * N_MP],
    )


def solution(mesh):
    in_specs = (
        P("dp", "mp"),
        P("dp", "mp"),
        P("dp", "mp"),
        P("dp", "mp"),
        P("dp", "mp"),
        P("mp"),
        P("mp"),
        P(),
        P("mp", None),
        P("dp", None),
    )
    out_specs = (P("mp", None), P(), P())
    return jax.shard_map(
        per_device, mesh=mesh, in_specs=in_specs, out_specs=out_specs, check_vma=False
    )
```

```python
import functools

import jax
import jax.numpy as jnp
from jax import lax
from jax.experimental import pallas as pl
from jax.experimental.pallas import tpu as pltpu
from jax.sharding import PartitionSpec as P

EPS = 1e-06
F32 = jnp.float32
BF16 = jnp.bfloat16
HIGH = lax.Precision.HIGHEST
TOK = 128
HD = 128
HEADS = 2
REPS = 64
N_Z = 16
N_Y = 4
N_MP = 8
PAIR = 2 * N_Y
N_PAIRS = N_Z // 2
ROWS = 32
COLS = 256
PITCH = 36
LIMIT = 48 * 1024 * 1024
NN = (((1,), (0,)), ((), ()))
NT = (((1,), (1,)), ((), ()))

Z_GROUPS = [[z * N_Y + y for z in range(N_Z)] for y in range(N_Y)]
Z_ORDER = [int(f"{z:04b}"[::-1], 2) for z in range(N_Z)]
ORDER = [z * N_Y + y for z in Z_ORDER for y in range(N_Y)]
K_ORDER = [0, 4, 2, 6, 1, 5, 3, 7]
EVERY_OTHER = [
    [(2 * k + i) * N_Y + y for k in K_ORDER] for i in range(2) for y in range(N_Y)
]
PAIRS = [[k * PAIR + i for i in range(PAIR)] for k in range(N_PAIRS)]
PLANES = [[z * N_Y * N_MP + i for i in range(N_Y * N_MP)] for z in range(N_Z)]


def matmul(a, b, dims=NN):
    return lax.dot_general(a, b, dims, precision=HIGH, preferred_element_type=F32)


def matmul3(a, b, dims=NN):
    ah, bh = a.astype(BF16), b.astype(BF16)
    al, bl = (a - ah.astype(F32)).astype(BF16), (b - bh.astype(F32)).astype(BF16)
    dot = functools.partial(lax.dot_general, dimension_numbers=dims, preferred_element_type=F32)
    return dot(ah, bh) + (dot(ah, bl) + dot(al, bh))


def places(shape):
    return (
        lax.broadcasted_iota(jnp.int32, shape, 0),
        lax.broadcasted_iota(jnp.int32, shape, 1),
    )


def unit_rows(raw):
    value = raw.astype(F32)
    return value / jnp.sqrt(jnp.sum(value * value, axis=-1, keepdims=True) + EPS)


def within(shift):
    row, col = places((TOK, TOK))
    return (row >> shift) == (col >> shift)


def invert_blocks(systems, mul):
    eye = within(0).astype(F32)
    first = [jnp.where(within(3), low, 0.0) for low in systems]
    second = [mul(a, a) for a in first]
    out = [eye - a for a in first]
    fourth = [mul(a, a) for a in second]
    out = [a + mul(a, b) for a, b in zip(out, second)]
    return [a + mul(a, b) for a, b in zip(out, fourth)]


def widen(systems, inverses, given, shift, mul):
    rest = within(shift + 2) & ~within(shift)
    steps = [mul(a, jnp.where(rest, low, 0.0)) for low, a in zip(systems, inverses)]
    out = inverses if given is None else [mul(a, v) for a, v in zip(inverses, given)]
    squares = [mul(a, a) for a in steps]
    out = [v - mul(a, v) for a, v in zip(steps, out)]
    return [v + mul(a, v) for a, v in zip(squares, out)]


def solve_all(systems, given, mul=matmul):
    inverses = widen(systems, invert_blocks(systems, mul), None, 3, mul)
    return widen(systems, inverses, given, 5, mul)


def small_inputs(dec_ref, beta_ref, rate_ref, bias_ref):
    row, col = places((TOK, TOK))
    falls = []
    for h in range(HEADS):
        pre = dec_ref[h : h + 1, :] + bias_ref[:, h : h + 1]
        soft = jnp.maximum(pre, 0.0) + jnp.log1p(jnp.exp(-jnp.abs(pre)))
        falls.append(-jnp.exp(rate_ref[:, h : h + 1]) * soft)
    cumul = matmul(jnp.concatenate(falls, axis=0), (row <= col).astype(F32))
    return cumul, 1.0 / (1.0 + jnp.exp(-beta_ref[...]))


def delta_parts(cumul, beta, inner, scores):
    row, col = places((TOK, TOK))
    lower = row >= col
    strict = row > col
    mixers, systems, spreads, strengths = [], [], [], []
    for h in range(HEADS):
        wide = jnp.broadcast_to(cumul[h : h + 1, :], (TOK, TOK))
        spread = jnp.where(lower, wide.T - wide, 0.0)
        decay = jnp.where(lower, jnp.exp(spread), 0.0)
        strength = jnp.broadcast_to(beta[h : h + 1, :], (TOK, TOK)).T
        mixers.append(scores * decay)
        systems.append(jnp.where(strict, strength * inner * decay, 0.0))
        spreads.append(spread)
        strengths.append(strength)
    return mixers, systems, spreads, strengths


def forward_kernel(
    k_any, q_any, v_any, up_any, dec_ref, beta_ref, rate_ref, bias_ref, gain_ref,
    g_any, k_ref, q_ref, v_ref, up_ref, g_ref, in_sems, out_sems,
):
    pairs = ((k_any, k_ref), (q_any, q_ref), (v_any, v_ref), (up_any, up_ref))
    fetches = [pltpu.make_async_copy(a, b, in_sems.at[i]) for i, (a, b) in enumerate(pairs)]
    for fetch in fetches:
        fetch.start()
    cumul, beta = small_inputs(dec_ref, beta_ref, rate_ref, bias_ref)
    heads = range(HEADS)
    fetches[0].wait()
    keys = unit_rows(k_ref[...])
    inner = matmul3(keys, keys, NT)
    fetches[1].wait()
    scores = matmul3(unit_rows(q_ref[...]) * HD ** (-0.5), keys, NT)
    mixers, systems, _, strengths = delta_parts(cumul, beta, inner, scores)
    fetches[2].wait()
    scaled = [strengths[h] * v_ref[:, h * HD : (h + 1) * HD].astype(F32) for h in heads]
    writes = solve_all(systems, scaled, matmul3)
    mixed = [matmul3(mixers[h], writes[h]) for h in heads]
    normed = []
    for h in heads:
        scale = lax.rsqrt(jnp.mean(mixed[h] * mixed[h], axis=-1, keepdims=True) + EPS)
        normed.append((mixed[h] * scale * gain_ref[...]).T.astype(BF16))
    left = jnp.concatenate(normed, axis=0)
    fetches[3].wait()
    stores = []
    for k in range(N_PAIRS):
        part = lax.dot_general(
            left, up_ref[:, k * COLS : (k + 1) * COLS], NN, preferred_element_type=F32
        ).astype(BF16)
        for i in range(2):
            z = 2 * k + i
            slot = Z_ORDER.index(z) * N_Y
            for y in range(N_Y):
                g_ref[slot + y] = part[(i * N_Y + y) * ROWS : (i * N_Y + y + 1) * ROWS, :]
            tiles = pl.ds(slot, N_Y)
            stores.append(pltpu.make_async_copy(g_ref.at[tiles], g_any.at[tiles], out_sems.at[z]))
            stores[z].start()
    for store in stores:
        store.wait()


def backward_kernel(
    place_ref, k_any, q_any, v_any, up_any, weight_any, _, dec_ref, beta_ref, rate_ref, bias_ref,
    gain_ref, out_ref, k_ref, q_ref, v_ref, up_ref, weight_ref, in_sems,
):
    pairs = (
        (k_any, k_ref), (q_any, q_ref), (v_any, v_ref), (up_any, up_ref), (weight_any, weight_ref)
    )
    fetches = [pltpu.make_async_copy(a, b, in_sems.at[i]) for i, (a, b) in enumerate(pairs)]
    for fetch in fetches:
        fetch.start()
    for fetch in fetches:
        fetch.wait()
    gain = gain_ref[...]
    d_normed = lax.dot_general(up_ref[...], weight_ref[...], NT, preferred_element_type=F32)
    lane = lax.broadcasted_iota(jnp.int32, (1, HD), 1)
    heads = range(HEADS)
    keys = unit_rows(k_ref[...])
    inner = matmul(keys, keys, NT)
    scores = matmul(unit_rows(q_ref[...]) * HD ** (-0.5), keys, NT)
    cumul, beta = small_inputs(dec_ref, beta_ref, rate_ref, bias_ref)
    mixers, systems, spreads, strengths = delta_parts(cumul, beta, inner, scores)
    scaled = [strengths[h] * v_ref[:, h * HD : (h + 1) * HD].astype(F32) for h in heads]
    writes = solve_all(systems, scaled)
    outs = [matmul(mixers[h], writes[h]) for h in heads]
    turns = solve_all(systems, [matmul(systems[h] * spreads[h], writes[h]) for h in heads])
    slopes = [
        matmul(mixers[h] * spreads[h], writes[h]) - matmul(mixers[h], turns[h]) for h in heads
    ]
    grad_gain = jnp.zeros((1, HD), F32)
    rates = jnp.zeros((1, HD), F32)
    for h in heads:
        mixed = outs[h]
        scale = lax.rsqrt(jnp.mean(mixed * mixed, axis=-1, keepdims=True) + EPS)
        unit = mixed * scale
        given = d_normed[:, h * HD : (h + 1) * HD]
        grad_gain = grad_gain + jnp.sum(unit * given, axis=0, keepdims=True)
        tilted = given * gain
        d_mixed = scale * (tilted - unit * jnp.mean(unit * tilted, axis=-1, keepdims=True))
        rate = jnp.sum(jnp.sum(d_mixed * slopes[h], axis=0, keepdims=True), axis=1, keepdims=True)
        rates = rates + jnp.where(lane == place_ref[0] * HEADS + h, rate, 0.0)
    out_ref[...] = jnp.concatenate([grad_gain, rates], axis=0)


def turn_left(value):
    row, _ = places(value.shape)
    parts = []
    for g in range(REPS // 8):
        part = value[8 * g : 8 * g + 8]
        parts.append(pltpu.roll(part, HD - 8 * g, 1) if g else part)
    value = jnp.concatenate(parts, axis=0)
    for bit in range(3):
        value = jnp.where((row >> bit) & 1 == 1, pltpu.roll(value, HD - 2**bit, 1), value)
    return value


def turn_right(value):
    parts = [
        pltpu.roll(value[8 * g : 8 * g + 8], 8 * g, 1, stride=1, stride_axis=0)
        for g in range(REPS // 8)
    ]
    return jnp.concatenate(parts, axis=0)


def twice(value):
    return jnp.concatenate([value, value], axis=1)


def pack_gram(total):
    row, lane = places((REPS, HD))
    wide = twice(total)
    turned = turn_left(wide)
    _, slot = places((16, HD))
    packed = turned[0:16]
    for q in range(1, 4):
        packed = jnp.where(
            slot >> 5 == q, pltpu.roll(turned[16 * q : 16 * q + 16], 32 * q, 1), packed
        )
    across = (lane < REPS) & (row == (lane + 32) & (REPS - 1))
    return packed, jnp.sum(jnp.where(across, wide, 0.0), axis=0, keepdims=True)


def unpack_gram(packed, last):
    row, lane = places((REPS, HD))
    turned = jnp.concatenate(
        [packed] + [pltpu.roll(packed, HD - 32 * q, 1) for q in range(1, 4)], axis=0
    )
    upper = turn_right(jnp.where(lane < 32, turned, 0.0))
    upper = upper + pltpu.roll(upper, REPS, 1)
    col = lane & (REPS - 1)
    other = jnp.where(row == col, 0.0, twice(upper[:, :REPS].T))
    half = last + pltpu.roll(last, REPS, 1)
    return upper + other + jnp.where(row == (col + 32) & (REPS - 1), half, 0.0)


def gram_kernel(place_ref, x_ref, small_ref, out_ref, wide):
    for e in range(2):
        for r in range(REPS):
            wide[e, pl.ds(ORDER[r] * PITCH, ROWS), :] = x_ref[r, :, e * HD : (e + 1) * HD].astype(F32)
    total = jnp.zeros((REPS, REPS), F32)
    for f in range(ROWS):
        rows = jnp.concatenate(
            [wide[e, pl.ds(f, REPS, stride=PITCH), :].astype(BF16) for e in range(2)], axis=1
        )
        total = total + lax.dot_general(rows, rows, NT, preferred_element_type=F32)
    packed, last = pack_gram(total)
    own = [place_ref[0] == y for y in range(N_Y)]
    high, low = split(small_ref[...])
    rate = high[1:2] + pltpu.roll(low[1:2], REPS, 1)
    rates = jnp.where(own[0], rate, 0.0)
    for y in range(1, N_Y):
        rates = jnp.where(own[y], pltpu.roll(rate, 16 * y, 1), rates)
    gains = [jnp.where(own[y], part[0:1], 0.0) for part in (high, low) for y in range(N_Y)]
    block = jnp.concatenate([packed, last, rates, *gains, jnp.zeros((6, HD), F32)], axis=0)
    out_ref[...] = jnp.broadcast_to(block.astype(BF16)[None], out_ref.shape)


def split(value):
    high = value.astype(BF16).astype(F32)
    return high, value - high


def spread_kernel(in_ref, out_ref):
    total = in_ref[0].astype(F32)
    for m in range(1, N_Y * N_MP):
        total = total + in_ref[m].astype(F32)
    lane = lax.broadcasted_iota(jnp.int32, (1, HD), 1)
    rates = total[17:18] + pltpu.roll(total[17:18], REPS, 1)
    high, low = split(jnp.concatenate([rates, total[18:22] + total[22:26]], axis=0))
    rates = jnp.where(lane < REPS, high[0:1], low[0:1])
    block = jnp.concatenate(
        [total[0:17], rates, high[1:5], low[1:5], jnp.zeros((6, HD), F32)], axis=0
    )
    out_ref[...] = jnp.broadcast_to(block.astype(BF16)[None], out_ref.shape)


def small_tree(stack):
    half = REPS // 2
    while half:
        other = pltpu.roll(stack, half, 0)
        inner = jnp.sum(stack * other, axis=1, keepdims=True)
        norm = jnp.sum(stack * stack, axis=1, keepdims=True)
        part = (1.0 - inner / (2.0 * (norm + EPS))) * stack
        stack = part + pltpu.roll(part, half, 0)
        half //= 2
    return stack[0:1]


def trees_kernel(in_ref, gain_ref, rate_ref):
    lane = lax.broadcasted_iota(jnp.int32, (1, HD), 1)
    gains, rates = [], []
    for z in range(N_Z):
        block = in_ref[z].astype(F32)
        gains.append(block[18:22] + block[22:26])
        row = block[17:18]
        row = row + pltpu.roll(row, REPS, 1)
        for y in range(N_Y):
            rates.append(jnp.where(lane < 16, pltpu.roll(row, (-16 * y) % HD, 1), 0.0))
    gain_ref[...] = small_tree(jnp.concatenate(gains, axis=0))
    rate_ref[...] = small_tree(jnp.concatenate(rates, axis=0))


def path_coefs(gram):
    row, lane = places((REPS, HD))
    col = lane & (REPS - 1)
    first = lane < REPS

    def ratio(inner, norm):
        return 1.0 - inner / (2.0 * (norm + EPS))

    def pick(mask, axis):
        return jnp.sum(jnp.where(mask, gram, 0.0), axis=axis, keepdims=True)

    coefs = jnp.ones((REPS, 1), F32)
    half = REPS // 2
    same = row == col
    while half:
        across = row == (col + half) & (REPS - 1)
        by_col = ratio(pick(across & first, 1), pick(same & first, 1))
        by_row = ratio(pick(across, 0), pick(same, 0))
        coefs = coefs * by_col
        part = by_col * by_row * gram
        part = part + pltpu.roll(part, half, 1)
        gram = part + pltpu.roll(part, half, 0)
        half //= 2
    return coefs


def combine_kernel(in_ref, x_ref, out_ref, factor):
    total = in_ref[0].astype(F32)
    for z in range(1, N_Z):
        total = total + in_ref[z].astype(F32)
    gram = unpack_gram(total[0:16], total[16:17])
    factor[...] = jnp.broadcast_to(path_coefs(gram), (REPS, COLS))
    total = jnp.zeros((ROWS, COLS), F32)
    for r in range(REPS):
        total = total + factor[ORDER[r] : ORDER[r] + 1, :] * x_ref[r].astype(F32)
    out_ref[...] = jnp.broadcast_to(total.astype(BF16)[None], out_ref.shape)


def unfold_kernel(in_ref, out_any, line_ref, sems):
    for i, k in enumerate(K_ORDER):
        line_ref[:, k * COLS : (k + 1) * COLS] = in_ref[i]
    stores = [pltpu.make_async_copy(line_ref, out_any.at[i], sems.at[i]) for i in range(PAIR)]
    for store in stores:
        store.start()
    for store in stores:
        store.wait()


def unfold(tiles):
    (out,) = call(
        unfold_kernel,
        [shape((PAIR, ROWS, N_PAIRS * COLS), BF16)],
        [tiles],
        scratch=[pltpu.VMEM((ROWS, N_PAIRS * COLS), BF16), pltpu.SemaphoreType.DMA((PAIR,))],
        out_hbm=(0,),
    )
    return out


def call(body, outs, ops, scratch=(), smem=(), hbm=(), out_hbm=(), flops=0, limit=LIMIT):
    size = sum(o.size * o.dtype.itemsize for o in ops) + sum(o.size * o.dtype.itemsize for o in outs)
    spaces = [
        pltpu.SMEM if i in smem else pl.ANY if i in hbm else pltpu.VMEM for i in range(len(ops))
    ]
    return pl.pallas_call(
        body,
        out_shape=outs,
        in_specs=[pl.BlockSpec(memory_space=space) for space in spaces],
        out_specs=[
            pl.BlockSpec(memory_space=pl.ANY if i in out_hbm else pltpu.VMEM)
            for i in range(len(outs))
        ],
        scratch_shapes=list(scratch),
        compiler_params=pltpu.CompilerParams(vmem_limit_bytes=limit),
        cost_estimate=pl.CostEstimate(flops=flops, bytes_accessed=size, transcendentals=0),
    )(*ops)


def shape(dims, dtype=F32):
    return jax.ShapeDtypeStruct(dims, dtype)


def forward(big, rows, gain_row):
    (tiles,) = call(
        forward_kernel,
        [shape((REPS, ROWS, COLS), BF16)],
        [*big, *rows, gain_row],
        scratch=[pltpu.VMEM(a.shape, BF16) for a in big]
        + [
            pltpu.VMEM((REPS, ROWS, COLS), BF16),
            pltpu.SemaphoreType.DMA((4,)),
            pltpu.SemaphoreType.DMA((N_Z,)),
        ],
        hbm=(0, 1, 2, 3),
        out_hbm=(0,),
        limit=56 * 2**20,
        flops=2 * 10**9,
    )
    return tiles


def backward(place, big, tiles, rows, gain_row):
    (small,) = call(
        backward_kernel,
        [shape((2, HD))],
        [place, *big, tiles, *rows, gain_row],
        scratch=[pltpu.VMEM(a.shape, BF16) for a in big] + [pltpu.SemaphoreType.DMA((5,))],
        smem=(0,),
        hbm=(1, 2, 3, 4, 5, 6),
        limit=56 * 2**20,
        flops=2 * 10**9,
    )
    return small


def gram(stack, small, place):
    (part,) = call(
        gram_kernel,
        [shape((N_Y * N_MP, 32, HD), BF16)],
        [place, stack, small],
        scratch=[pltpu.VMEM((2, REPS * PITCH + 64, HD), F32)],
        smem=(0,),
        flops=10**9,
    )
    return part


def combine(packed, stack):
    (tile,) = call(
        combine_kernel,
        [shape((N_PAIRS, ROWS, COLS), BF16)],
        [packed, stack],
        scratch=[pltpu.VMEM((REPS, COLS), F32)],
        flops=10**8,
    )
    return tile


def per_device(
    query_raw, key_raw, values, decay_input, beta_input, log_rate, step_bias, gain, out_weight, upstream
):
    gain_row = gain[None, :]
    big = (key_raw, query_raw, values, upstream)
    rows = (decay_input.T, beta_input.T, log_rate[None, :], step_bias[None, :])
    tiles = forward(big, rows, gain_row)
    stack = lax.all_to_all(tiles, "dp", 0, 0, axis_index_groups=[ORDER])
    place = lax.axis_index("mp").astype(jnp.int32)[None]
    small = backward(place, (*big, out_weight), tiles, rows, gain_row)
    place = (lax.axis_index("dp") % N_Y).astype(jnp.int32)[None]
    part = gram(stack, small, place)
    part = lax.all_to_all(part, ("dp", "mp"), 0, 0, axis_index_groups=PLANES)
    (part,) = call(spread_kernel, [shape((N_Z, 32, HD), BF16)], [part])
    packed = lax.all_to_all(part, "dp", 0, 0, axis_index_groups=Z_GROUPS)
    whole = combine(packed, stack)
    whole = lax.all_to_all(whole, "dp", 0, 0, axis_index_groups=EVERY_OTHER)
    whole = unfold(whole)
    whole = lax.all_to_all(whole, "dp", 0, 0, axis_index_groups=PAIRS)
    gain_final, rate_final = call(
        trees_kernel, [shape((1, HD)), shape((1, HD))], [packed]
    )
    return (
        whole.reshape(PAIR * ROWS, N_PAIRS * COLS),
        gain_final[0],
        rate_final[0, : HEADS * N_MP],
    )


def solution(mesh):
    in_specs = (
        P("dp", "mp"),
        P("dp", "mp"),
        P("dp", "mp"),
        P("dp", "mp"),
        P("dp", "mp"),
        P("mp"),
        P("mp"),
        P(),
        P("mp", None),
        P("dp", None),
    )
    out_specs = (P("mp", None), P(), P())
    return jax.shard_map(
        per_device, mesh=mesh, in_specs=in_specs, out_specs=out_specs, check_vma=False
    )
```
